128 devices in a mesh: wave: 4 (over x), event: 32 (over z, y, core).
Axes of the slice: x: 4, y: 4, z: 4, core: 2. Of those that a mesh axis runs over, the one named last changes fastest.
Arguments:
- latent: bfloat16 [8, 512, 2048], P(None, 'wave', 'event'), may hold values from -6 to 6
- basis: bfloat16 [1048576, 512], P('event', 'wave'), may hold values from -0.29882812 to 0.29882812
- event_bin: int32 [32, 32768], P('event'), may hold values from 0 to 63, never falling along the last dimension, each value on 1 to 2048 neighbouring positions
- length: float32 [512, 2048], P('wave', 'event'), may hold values from 0.01 to 0.08
- amplitude_scale: float32 [512, 2048], P('wave', 'event'), may hold values from 0.3 to 1
- yield_norm: float32 [512, 2048], P('wave', 'event'), may hold values from 0.5 to 2
- bin_coords: float32 [2, 2048], replicated, may hold values from 0 to 1
Outputs:
- grad_latent: float32 [8, 512, 2048], P(None, 'wave', 'event')
The draws below stay inside these ranges and needn't reach their ends.
Inputs may be any that keep to these rules, and one draw needn't show every extreme that they name: `event_bin`: along each block's events, bin numbers never fall and every one of the block's bins holds at least one event.
All inputs are finite; a program needn't handle non-finite values.
Results may differ from the reference program's by a relative error of at most 0.0024.
Values may be sent and summed in bfloat16 or wider, within the bound.
No kernel may reach another device: no remote copies, remote signals or barrier semaphores. Data moves between devices by JAX's collectives and lax.ppermute only.
A program may use at most 128 MiB of HBM per device.

```python
import math
import jax
import jax.numpy as jnp
import numpy as np
from jax import lax

B = 2048
W = 512
S = 8
EV_DEV = 32768
NBLOCKS = 32
EVENTS = 1048576
N_EVENT = 32


def block_scale(own_key, shape, split, least, largest):
    def one(position, blocks):
        steps = jax.random.uniform(jax.random.fold_in(jax.random.fold_in(own_key, 6), position), (blocks,), jnp.float32, least / len(split), largest / len(split))
        return jnp.repeat(jnp.exp(steps), shape[position] // blocks).reshape((-1,) + (1,) * (len(shape) - position - 1))

    gain = one(*split[0])
    for cut in split[1:]:
        gain = gain * one(*cut)
    return gain


def length_profile(amount, total, most, lean):
    portions = [(1 << 20) // math.isqrt(grade ** lean) + 1 for grade in range(2, amount + 1)]
    spare, counts = total - most - (amount - 1), [1] * (amount - 1)
    while spare > 0:
        candidates = [i for i in range(amount - 1) if counts[i] < most]
        pool, budget = sum([portions[i] for i in candidates]), spare
        for i in candidates:
            addition = min(most - counts[i], max(1, budget * portions[i] // pool), spare)
            counts[i] = counts[i] + addition
            spare = spare - addition
    return np.array([most] + counts)


def uneven(stream_key, amount, total, bound, skew):
    if amount == 2:
        one = jax.random.randint(stream_key, (), max(1, total - bound), min(bound, total - 1) + 1)
        return jnp.stack([one, total - one])
    tallies = jnp.asarray(length_profile(amount, total, bound, skew), jnp.int32)
    couples = (amount - 1) // 2
    source_of, receiver = tallies[1:1 + 2 * couples:2], tallies[2:2 + 2 * couples:2]
    slack = jnp.minimum(source_of - 1, bound - receiver)
    passed = jax.random.randint(jax.random.fold_in(stream_key, 1), (couples,), 0, 1 << 20) % (slack + 1)
    tallies = tallies.at[1:1 + 2 * couples:2].set(source_of - passed).at[2:2 + 2 * couples:2].set(receiver + passed)
    return tallies[jax.random.permutation(jax.random.fold_in(stream_key, 2), amount)]


def gaussian(rng, dims, width, reach, cuts=(), held_as=jnp.bfloat16):
    factor_of = block_scale(rng, dims, cuts, -0.22, 0.18) if cuts else 1.0
    drawn = jax.random.normal(rng, dims, jnp.float32) * width * factor_of
    return jnp.minimum(jnp.maximum(drawn, -reach), reach).astype(held_as)


def setup_inputs(seed: int = 0) -> dict:
    key_of = jax.random.split(jax.random.key(seed), 8)
    return {
        "latent": gaussian(key_of[0], (S, W, B), 1.0, 6.0, ((1, 4), (2, 32))),
        "basis": gaussian(key_of[1], (EVENTS, W), 0.05, 0.29882812, ((0, 32), (1, 4))),
        "event_bin": jax.vmap(lambda own: jnp.searchsorted(jnp.cumsum(uneven(own, B // N_EVENT, EV_DEV, min(4 * EV_DEV // (B // N_EVENT), EV_DEV - B // N_EVENT + 1), 2)), jnp.arange(EV_DEV), side="right"))(jax.random.split(key_of[2], NBLOCKS)).reshape((NBLOCKS, EV_DEV)).astype(jnp.int32),
        "length": jnp.clip(jnp.exp(math.log(0.08) - 2.0794415 * jax.random.uniform(key_of[3], (W, B), jnp.float32) ** block_scale(key_of[3], (W, B), ((0, 4), (1, 32)), -0.2, 0.2)), 0.01, 0.08),
        "amplitude_scale": jnp.clip(jnp.exp(math.log(1.0) - 1.2039728 * jax.random.uniform(key_of[4], (W, B), jnp.float32) ** block_scale(key_of[4], (W, B), ((0, 4), (1, 32)), -0.2, 0.2)), 0.3, 1.0),
        "yield_norm": jnp.clip(jnp.exp(math.log(2.0) - 1.3862944 * jax.random.uniform(key_of[5], (W, B), jnp.float32) ** block_scale(key_of[5], (W, B), ((0, 4), (1, 32)), -0.2, 0.2)), 0.5, 2.0),
        "bin_coords": jnp.clip(jax.random.uniform(key_of[6], (2, B), jnp.float32, 0.0, 1.0), 0.0, 1.0),
    }


def gibbs(rows_xy, cols_xy, len_rows, amp_rows, len_cols, amp_cols):
    diff_x = rows_xy[0][:, None] - cols_xy[0][None, :]
    diff_y = rows_xy[1][:, None] - cols_xy[1][None, :]
    dist = diff_x * diff_x + diff_y * diff_y
    left = len_rows[:, :, None]
    right = len_cols[:, None, :]
    spread = left * left + right * right
    return amp_rows[:, :, None] * amp_cols[:, None, :] * jnp.sqrt(2.0 * (left * right) / spread) * jnp.exp(-dist / spread)

def reference(latent, basis, event_bin, length, amplitude_scale, yield_norm, bin_coords):
    rows = B // N_EVENT

    def wave_kernel(w_index):
        len_wave = length[w_index][None]
        amp_wave = amplitude_scale[w_index][None]
        return gibbs(bin_coords, bin_coords, len_wave, amp_wave, len_wave, amp_wave)[0].astype(jnp.bfloat16)

    def forward_wave(w_index):
        kern = wave_kernel(w_index)
        return jnp.dot(kern, latent[:, w_index, :].T, preferred_element_type=jnp.float32)
    amps = lax.map(forward_wave, jnp.arange(W, dtype=jnp.int32))
    amplitude = jnp.transpose(amps, (2, 0, 1)).astype(jnp.bfloat16)
    basis_blocks = basis.reshape(NBLOCKS, EV_DEV, W)

    def block_sums(pieces):
        blk, psi, seg = pieces
        local = lax.dynamic_slice_in_dim(amplitude, (blk * rows).astype(jnp.int32), rows, 2).astype(jnp.float32)
        picked = jnp.transpose(local, (2, 0, 1))[seg]
        psi_wide = psi.astype(jnp.float32)
        field = lax.optimization_barrier(jnp.sum(picked * psi_wide[:, None, :], axis=2))
        weight = -2.0 * field / (1.0 + field * field) / S
        terms = (weight[:, :, None] * psi_wide[:, None, :]).astype(jnp.bfloat16)
        terms = lax.optimization_barrier(terms).astype(jnp.float32)
        return jax.ops.segment_sum(terms, seg, num_segments=rows)
    sums = lax.map(block_sums, (jnp.arange(NBLOCKS, dtype=jnp.int32), basis_blocks, event_bin))
    sums = sums.reshape(B, S, W)
    yield_term = 2.0 / S * amplitude.astype(jnp.float32) * yield_norm[None]
    bin_grad = (sums + jnp.transpose(yield_term, (2, 0, 1))).astype(jnp.bfloat16)

    def backward_wave(w_index):
        kern = wave_kernel(w_index)
        return jnp.dot(kern, bin_grad[:, :, w_index], preferred_element_type=jnp.float32)
    grads = lax.map(backward_wave, jnp.arange(W, dtype=jnp.int32))
    return jnp.transpose(grads, (2, 0, 1)) + latent.astype(jnp.float32)
```

```python
import math

import jax
import jax.numpy as jnp
from jax import lax
from jax.experimental import pallas as pl
from jax.experimental.pallas import tpu as pltpu
from jax.sharding import PartitionSpec as P

F32 = jnp.float32
BF16 = jnp.bfloat16

S, WL, R, B, E, G, NW = 8, 128, 64, 2048, 32768, 32, 4
NX = 4
TB = 256
NB = B // TB
NT = NB + NB * (NB - 1) // 2
IN_ROWS = 24
T = 512
Q = E // NX
HQ = Q // 2
NWIN = 8
ROOT = math.sqrt(math.log2(math.e))
VMEM = pl.BlockSpec(memory_space=pltpu.VMEM)
SMEM = pl.BlockSpec(memory_space=pltpu.SMEM)
ANY = pl.BlockSpec(memory_space=pl.ANY)
PARAMS = pltpu.CompilerParams(vmem_limit_bytes=56 * 1024 * 1024)


def low_lanes(shape):
    return lax.broadcasted_iota(jnp.int32, shape, len(shape) - 1) < 64


def swap(x):
    return pltpu.roll(x, 64, 1)


def pack_kernel(lat_ref, len_ref, amp_ref, out_ref):
    def rows(ref, qh):
        a = ref[pl.ds(qh * G, G), :]
        b = ref[pl.ds((qh + 2) * G, G), :]
        return jnp.concatenate([a.astype(F32), b.astype(F32)], axis=1)

    for qh in range(2):
        for s in range(S):
            out_ref[pl.ds(qh * S + s, G, stride=IN_ROWS), :] = rows(lat_ref.at[s], qh)
        out_ref[pl.ds(16 + qh * 2, G, stride=IN_ROWS), :] = rows(len_ref, qh)
        out_ref[pl.ds(17 + qh * 2, G, stride=IN_ROWS), :] = rows(amp_ref, qh)
    for r in range(20, IN_ROWS):
        out_ref[pl.ds(r, G, stride=IN_ROWS), :] = jnp.zeros((G, 128), F32)


def split_pair(a, b):
    low = low_lanes(a.shape)
    return jnp.where(low, a, swap(b)), jnp.where(low, swap(a), b)


def put_vectors(x_ref, q, k, vec):
    hi = vec.astype(BF16)
    lo = (vec - hi.astype(F32)).astype(BF16)
    x_ref[q, k // 2, :, (k % 2) * 128 : (k % 2) * 128 + 128] = jnp.concatenate([hi, lo], axis=0)


def times_tile(x_ref, y_ref, q, i, j, tile, both):
    y_ref[q, j] += jnp.dot(x_ref[q, i], tile, preferred_element_type=F32)
    if both:
        y_ref[q, i] += lax.dot_general(
            x_ref[q, j], tile, (((1,), (1,)), ((), ())), preferred_element_type=F32
        )


def tile_place(t):
    i = t & (NB - 1)
    return i, (i + (t >> 3)) & (NB - 1)


def send_rows(y_ref, scale_ref, out_ref):
    for k in range(B // 128):
        def part(q):
            y = y_ref[q, k // 2, :, (k % 2) * 128 : (k % 2) * 128 + 128]
            return (y[0:8] + y[8:16]) * scale_ref[q : q + 1, k * 128 : k * 128 + 128]

        first, second = [], []
        for qh in range(2):
            a, b = split_pair(part(qh), part(qh + 2))
            first.append(a)
            second.append(b)
        out_ref[32 * k : 32 * k + 16, :] = jnp.concatenate(first, axis=0).astype(out_ref.dtype)
        out_ref[32 * k + 16 : 32 * k + 32, :] = jnp.concatenate(second, axis=0).astype(out_ref.dtype)


def gen_kernel(r_ref, xy_ref, kern_ref, amp_ref, scale_ref, store, la, x_ref, y_ref, sq_row, sq_col, xy_row, xy_col, dist, sem):
    scale_ref[...] = jnp.zeros_like(scale_ref)
    for k in range(B // 128):
        lanes = slice(k * 128, k * 128 + 128)
        base = 2 * k * IN_ROWS
        pair = split_pair(r_ref[base + 16 : base + 24, :], r_ref[base + IN_ROWS + 16 : base + IN_ROWS + 24, :])
        for h in range(2):
            la[h, :, lanes] = pair[h]
        for c in range(2):
            row = xy_ref[c : c + 1, lanes] * ROOT
            wide = jnp.broadcast_to(row, (128, 128))
            xy_row[c, k // 2, :, (k % 2) * 128 : (k % 2) * 128 + 128] = wide[0:8]
            xy_col[c, lanes, :] = wide.T
    for h in range(2):
        for qh in range(2):
            q = qh + 2 * h
            length = la[h, 2 * qh : 2 * qh + 1, :]
            amp = la[h, 2 * qh + 1 : 2 * qh + 2, :]
            scale_ref[q : q + 1, :] = amp * jnp.sqrt(length * math.sqrt(2.0))
            la[h, 2 * qh : 2 * qh + 1, :] = length * length
    for k in range(B // 128):
        lanes = slice(k * 128, k * 128 + 128)
        base = 2 * k * IN_ROWS
        for qh in range(2):
            pair = split_pair(
                r_ref[base + 8 * qh : base + 8 * qh + 8, :],
                r_ref[base + IN_ROWS + 8 * qh : base + IN_ROWS + 8 * qh + 8, :],
            )
            for h in range(2):
                q = qh + 2 * h
                put_vectors(x_ref, q, k, pair[h] * scale_ref[q : q + 1, lanes])
                wide = jnp.broadcast_to(la[h, 2 * qh : 2 * qh + 1, lanes], (128, 128))
                sq_row[q, k // 2, :, (k % 2) * 128 : (k % 2) * 128 + 128] = wide[0:8]
                sq_col[q, lanes, :] = wide.T
    y_ref[...] = jnp.zeros_like(y_ref)

    step = 32

    def tile(t, both):
        i, j = tile_place(t)
        row0 = pl.multiple_of(i * TB, TB)
        for st in range(TB // step):
            rows = pl.ds(row0 + st * step, step)
            xc = xy_col[0, rows, :].reshape(step // 8, 8, 128)
            yc = xy_col[1, rows, :].reshape(step // 8, 8, 128)
            for c in range(2):
                half = slice(c * 128, c * 128 + 128)
                dx = xc - xy_row[0, j, :, half][None]
                dy = yc - xy_row[1, j, :, half][None]
                d = -(dx * dx) - dy * dy
                dist[st * step : st * step + step, half] = d.reshape(step, 128)
        for q in range(NW):
            for st in range(TB // step):
                sq = sq_col[q, pl.ds(row0 + st * step, step), :].reshape(step // 8, 8, 128)
                parts = []
                for c in range(2):
                    half = slice(c * 128, c * 128 + 128)
                    root = lax.rsqrt(sq + sq_row[q, j, :, half][None])
                    d = dist[st * step : st * step + step, half].reshape(step // 8, 8, 128)
                    parts.append((root * jnp.exp2(root * root * d)).reshape(step, 128).astype(BF16))
                store[t, q, st * step : st * step + step, :] = jnp.concatenate(parts, axis=1)
            times_tile(x_ref, y_ref, q, i, j, store[t, q], both)
        pltpu.make_async_copy(store.at[t], kern_ref.at[t], sem).start()

    @pl.loop(0, NB)
    def _(t):
        tile(t, False)

    @pl.loop(NB, NT)
    def _(t):
        tile(t, True)

    send_rows(y_ref, scale_ref, amp_ref)
    pltpu.make_async_copy(store, kern_ref, sem).wait()


def pull_kernel(g_ref, scale_ref, kern_ref, out_ref, store, x_ref, y_ref, sems):
    for t in range(NT):
        pltpu.make_async_copy(kern_ref.at[t], store.at[t], sems.at[t]).start()
    for k in range(B // 128):
        lanes = slice(k * 128, k * 128 + 128)
        a = g_ref[32 * k : 32 * k + 16, :].astype(F32)
        b = g_ref[32 * k + 16 : 32 * k + 32, :].astype(F32)
        pair = split_pair(a, b)
        for h in range(2):
            for qh in range(2):
                q = qh + 2 * h
                put_vectors(x_ref, q, k, pair[h][8 * qh : 8 * qh + 8] * scale_ref[q : q + 1, lanes])
    y_ref[...] = jnp.zeros_like(y_ref)

    def tile(t, both):
        i, j = tile_place(t)
        pltpu.make_async_copy(kern_ref.at[t], store.at[t], sems.at[t]).wait()
        for q in range(NW):
            times_tile(x_ref, y_ref, q, i, j, store[t, q], both)

    @pl.loop(0, NB)
    def _(t):
        tile(t, False)

    @pl.loop(NB, NT)
    def _(t):
        tile(t, True)

    send_rows(y_ref, scale_ref, out_ref)


def window_bins(first, shape):
    return first + lax.broadcasted_iota(jnp.int32, shape, 0)


def forward_kernel(me_ref, bins_ref, seg_ref, amp_ref, basis_ref, out0, out1, out2, out3, rows_ref, table, psi, acc, sems):
    me = me_ref[0]

    def place(k, m):
        return pl.multiple_of(((me + k) & (NX - 1)) * Q + m * 1024, 1024)

    def copies(k, m):
        return [
            pltpu.make_async_copy(
                basis_ref.at[pl.ds(place(k, m) + half * HQ, 1024), :],
                psi.at[k * 4 + m, pl.ds(half * 1024, 1024), :],
                sems.at[k * 4 + m, half],
            )
            for half in range(2)
        ]

    @pl.loop(0, 16)
    def _(c):
        for one in copies(c >> 2, c & 3):
            one.start()

    rows_ref[...] = amp_ref[...].astype(F32)
    table[...] = jnp.zeros_like(table)
    low = low_lanes((64, 128))
    for s in range(0, S, 2):
        stack = [rows_ref[pl.ds(qh * S + s + d, G, stride=16), :] for d in range(2) for qh in range(2)]
        flipped = jnp.concatenate(stack, axis=0).T
        top, bottom = flipped[0:64], flipped[64:128]
        table[pl.ds(s, R, stride=S), :] = jnp.where(low, top, swap(bottom))
        table[pl.ds(s + 1, R, stride=S), :] = jnp.where(low, swap(top), bottom)

    for k, out_ref in enumerate((out0, out1, out2, out3)):

        @pl.loop(0, 4)
        def _(m):
            c = k * 4 + m
            for one in copies(k, m):
                one.wait()
            places = [(u, half, place(k, m) + half * HQ + u * T) for u in range(2) for half in range(2)]

            def select(u, half, event, first, start):
                window = table[pl.ds(pl.multiple_of(first * S, S), NWIN * S), :].astype(BF16)
                values = psi[c, half * 1024 + u * T : half * 1024 + u * T + T, :]
                fields = lax.dot_general(
                    window, values, (((1,), (1,)), ((), ())), preferred_element_type=F32
                )
                seg = jnp.broadcast_to(seg_ref[0:1, pl.ds(pl.multiple_of(event, T), T)], (S, T)) - first
                for g in range(NWIN):
                    start = jnp.where(seg == g, fields[g * S : g * S + S], start)
                return start

            spans = []
            for u, half, event in places:
                first = bins_ref[0, event]
                acc[u, half * S : half * S + S, :] = select(u, half, event, first, jnp.zeros((S, T), F32))
                spans.append(bins_ref[0, event + T - 1] - first)
            widest = jnp.maximum(jnp.maximum(spans[0], spans[1]), jnp.maximum(spans[2], spans[3]))

            @pl.when(widest >= NWIN)
            def _():
                for (u, half, event), span in zip(places, spans):
                    first = bins_ref[0, event]

                    @pl.loop(1, span // NWIN + 1)
                    def _(w):
                        old = acc[u, half * S : half * S + S, :]
                        acc[u, half * S : half * S + S, :] = select(u, half, event, first + w * NWIN, old)

            for u in range(2):
                out_ref[:, pl.ds(pl.multiple_of(m * 1024 + u * T, T), T)] = acc[u].astype(BF16)


def weight_kernel(a_ref, b_ref, c_ref, d_ref, out_ref):
    field = (a_ref[...].astype(F32) + b_ref[...].astype(F32)) + (c_ref[...].astype(F32) + d_ref[...].astype(F32))
    out_ref[...] = (-2.0 / S * field / (1.0 + field * field)).astype(BF16)


def backward_kernel(me_ref, bins_ref, w0_ref, w1_ref, w2_ref, w3_ref, seg_ref, amp_ref, norm_ref, basis_ref, out_ref, rows_ref, sums, psi, sems):
    me = me_ref[0]

    def place(k, m):
        return pl.multiple_of(((me - k) & (NX - 1)) * Q + m * 1024, 1024)

    def copies(k, m):
        return [
            pltpu.make_async_copy(
                basis_ref.at[pl.ds(place(k, m) + half * HQ, 1024), :],
                psi.at[k * 4 + m, pl.ds(half * 1024, 1024), :],
                sems.at[k * 4 + m, half],
            )
            for half in range(2)
        ]

    @pl.loop(0, 16)
    def _(c):
        for one in copies(c >> 2, c & 3):
            one.start()

    sums[...] = jnp.zeros_like(sums)
    for k, w_ref in enumerate((w0_ref, w1_ref, w2_ref, w3_ref)):

        @pl.loop(0, 4)
        def _(m):
            c = k * 4 + m
            for one in copies(k, m):
                one.wait()
            places = [(u, half, place(k, m) + half * HQ + u * T) for u in range(2) for half in range(2)]

            def add(u, half, event, first):
                weight = w_ref[:, pl.ds(pl.multiple_of(m * 1024 + u * T, T), T)].astype(F32)
                weight = weight[half * S : half * S + S]
                values = psi[c, half * 1024 + u * T : half * 1024 + u * T + T, :]
                seg = jnp.broadcast_to(seg_ref[0:1, pl.ds(pl.multiple_of(event, T), T)], (S, T)) - first
                spread = jnp.concatenate([jnp.where(seg == g, weight, 0.0) for g in range(NWIN)], axis=0)
                added = jnp.dot(spread.astype(BF16), values, preferred_element_type=F32)
                sums[pl.ds(pl.multiple_of(first * S, S), NWIN * S), :] += added

            spans = []
            for u, half, event in places:
                first = bins_ref[0, event]
                add(u, half, event, first)
                spans.append(bins_ref[0, event + T - 1] - first)
            widest = jnp.maximum(jnp.maximum(spans[0], spans[1]), jnp.maximum(spans[2], spans[3]))

            @pl.when(widest >= NWIN)
            def _():
                for (u, half, event), span in zip(places, spans):
                    first = bins_ref[0, event]

                    @pl.loop(1, span // NWIN + 1)
                    def _(w):
                        add(u, half, event, first + w * NWIN)

    rows_ref[...] = amp_ref[...].astype(F32)
    norm = [
        jnp.concatenate([norm_ref[pl.ds(qh * G, G), :], norm_ref[pl.ds((qh + 2) * G, G), :]], axis=1) * (2.0 / S)
        for qh in range(2)
    ]
    low = low_lanes((G, 128))
    for s in range(0, S, 2):
        stack = [sums[pl.ds(s + d, R, stride=S), :] for d in range(2)]
        flipped = jnp.concatenate(stack, axis=0).T
        for qh in range(2):
            a, b = flipped[qh * G : qh * G + G], flipped[(qh + 2) * G : (qh + 2) * G + G]
            parts = (jnp.where(low, a, swap(b)), jnp.where(low, swap(a), b))
            for d in range(2):
                where = pl.ds(qh * S + s + d, G, stride=16)
                rows_ref[where, :] = rows_ref[where, :] * norm[qh] + parts[d]
    out_ref[...] = rows_ref[...].astype(BF16)


def unpack_kernel(r_ref, lat_ref, out_ref):
    for qh in range(2):
        for s in range(S):
            v = r_ref[pl.ds(qh * S + s, G, stride=16), :]
            for h in range(2):
                where = pl.ds((qh + 2 * h) * G, G)
                out_ref[s, where, :] = v[:, h * 64 : h * 64 + 64] + lat_ref[s, where, :].astype(F32)


def struct(shape, dtype):
    return jax.ShapeDtypeStruct(shape, dtype)


def exchange(x, rows):
    y = lax.all_to_all(x.reshape(G, rows, 128), "event", 0, 0)
    return y.reshape(G * rows, 128)


def shift(x, k):
    return lax.ppermute(x, "wave", [(i, (i + k) % NX) for i in range(NX)])


def shards(latent, basis, event_bin, length, amplitude_scale, yield_norm, bin_coords):
    me = lax.axis_index("wave").astype(jnp.int32).reshape(1)
    packed = pl.pallas_call(
        pack_kernel,
        out_shape=struct((G * IN_ROWS, 128), F32),
        in_specs=[VMEM] * 3,
        out_specs=VMEM,
        name="pack",
    )(latent, length, amplitude_scale)
    arrived = exchange(packed, IN_ROWS)
    kern, amp_out, scale = pl.pallas_call(
        gen_kernel,
        out_shape=(
            struct((NT, NW, TB, TB), BF16),
            struct((G * 16, 128), BF16),
            struct((8, B), F32),
        ),
        in_specs=[VMEM] * 2,
        out_specs=(ANY, VMEM, VMEM),
        scratch_shapes=[
            pltpu.VMEM((NT, NW, TB, TB), BF16),
            pltpu.VMEM((2, 8, B), F32),
            pltpu.VMEM((NW, NB, 16, TB), BF16),
            pltpu.VMEM((NW, NB, 16, TB), F32),
            pltpu.VMEM((NW, NB, 8, TB), F32),
            pltpu.VMEM((NW, B, 128), F32),
            pltpu.VMEM((2, NB, 8, TB), F32),
            pltpu.VMEM((2, B, 128), F32),
            pltpu.VMEM((TB, TB), F32),
            pltpu.SemaphoreType.DMA,
        ],
        compiler_params=PARAMS,
        name="gen",
    )(arrived, bin_coords)
    amp_in = exchange(amp_out, 16)
    fields = pl.pallas_call(
        forward_kernel,
        out_shape=[struct((2 * S, HQ), BF16)] * NX,
        in_specs=[SMEM, SMEM, VMEM, VMEM, ANY],
        out_specs=[VMEM] * NX,
        scratch_shapes=[
            pltpu.VMEM((G * 16, 128), F32),
            pltpu.VMEM(((R + NWIN) * S, 128), F32),
            pltpu.VMEM((16, 2048, 128), BF16),
            pltpu.VMEM((2, 2 * S, T), F32),
            pltpu.SemaphoreType.DMA((16, 2)),
        ],
        compiler_params=PARAMS,
        name="forward",
    )(me, event_bin, event_bin, amp_in, basis)
    others = [shift(fields[k], k) for k in range(1, NX)]
    weight = pl.pallas_call(
        weight_kernel,
        out_shape=struct((2 * S, HQ), BF16),
        in_specs=[VMEM] * 4,
        out_specs=VMEM,
        name="weight",
    )(fields[0], *others)
    weights = [weight] + [shift(weight, k) for k in range(1, NX)]
    grad_out = pl.pallas_call(
        backward_kernel,
        out_shape=struct((G * 16, 128), BF16),
        in_specs=[SMEM, SMEM] + [VMEM] * 7 + [ANY],
        out_specs=VMEM,
        scratch_shapes=[
            pltpu.VMEM((G * 16, 128), F32),
            pltpu.VMEM(((R + NWIN) * S, 128), F32),
            pltpu.VMEM((16, 2048, 128), BF16),
            pltpu.SemaphoreType.DMA((16, 2)),
        ],
        compiler_params=PARAMS,
        name="backward",
    )(me, event_bin, *weights, event_bin, amp_in, yield_norm, basis)
    grad_in = exchange(grad_out, 16)
    pulled = pl.pallas_call(
        pull_kernel,
        out_shape=struct((G * 16, 128), F32),
        in_specs=[VMEM, VMEM, ANY],
        out_specs=VMEM,
        scratch_shapes=[
            pltpu.VMEM((NT, NW, TB, TB), BF16),
            pltpu.VMEM((NW, NB, 16, TB), BF16),
            pltpu.VMEM((NW, NB, 16, TB), F32),
            pltpu.SemaphoreType.DMA((NT,)),
        ],
        compiler_params=PARAMS,
        name="pull",
    )(grad_in, scale, kern)
    back = exchange(pulled, 16)
    return pl.pallas_call(
        unpack_kernel,
        out_shape=struct((S, WL, R), F32),
        in_specs=[VMEM] * 2,
        out_specs=VMEM,
        name="unpack",
    )(back, latent)


def solution(mesh):
    placed = (
        P(None, "wave", "event"),
        P("event", "wave"),
        P("event", None),
        P("wave", "event"),
        P("wave", "event"),
        P("wave", "event"),
        P(),
    )
    return jax.shard_map(
        shards, mesh=mesh, in_specs=placed, out_specs=P(None, "wave", "event"), check_vma=False
    )
```

```python
import math

import jax
import jax.numpy as jnp
from jax import lax
from jax.experimental import pallas as pl
from jax.experimental.pallas import tpu as pltpu
from jax.sharding import PartitionSpec as P

F32 = jnp.float32
BF16 = jnp.bfloat16

S, WL, R, B, E, G, NW = 8, 128, 64, 2048, 32768, 32, 4
NX = 4
SP = 4
TB = 256
NB = B // TB
NT = NB + NB * (NB - 1) // 2
IN_ROWS = 24
T = 512
TILES = E // T
Q = E // NX
HQ = Q // 2
NWIN = 8
ROOT = math.sqrt(math.log2(math.e))
VMEM = pl.BlockSpec(memory_space=pltpu.VMEM)
SMEM = pl.BlockSpec(memory_space=pltpu.SMEM)
ANY = pl.BlockSpec(memory_space=pl.ANY)


def low_lanes(shape):
    return lax.broadcasted_iota(jnp.int32, shape, len(shape) - 1) < 64


def swap(x):
    return pltpu.roll(x, 64, 1)


def pack_kernel(lat_hbm, len_hbm, amp_hbm, xy_hbm, out_ref, xy_ref, lat_ref, len_ref, amp_ref, rows, sems):
    copies = [
        pltpu.make_async_copy(source, target, sems.at[n])
        for n, (source, target) in enumerate(
            ((lat_hbm, lat_ref), (len_hbm, len_ref), (amp_hbm, amp_ref), (xy_hbm, xy_ref))
        )
    ]
    for one in copies:
        one.start()

    def put(row, value):
        for q in range(NW):
            rows[pl.ds(row(q), G, stride=IN_ROWS), :] = value[q * G : q * G + G]

    copies[0].wait()
    for sp in range(SP):
        pair = jnp.concatenate([lat_ref[sp], lat_ref[sp + SP]], axis=0).astype(F32)
        put(lambda q: q * SP + sp, pair.T)
    copies[1].wait()
    copies[2].wait()
    exact = jnp.concatenate([len_ref[...], amp_ref[...]], axis=0).T
    high = exact.astype(BF16).astype(F32)
    put(lambda q: 16 + q, high)
    put(lambda q: 20 + q, exact - high)
    out_ref[...] = rows[...].astype(BF16)
    copies[3].wait()


def split_pair(a, b):
    low = low_lanes(a.shape)
    return jnp.where(low, a, swap(b)), jnp.where(low, swap(a), b)


def put_vectors(x_ref, q, k, vec):
    hi = vec.astype(BF16)
    lo = (vec - hi.astype(F32)).astype(BF16)
    x_ref[q, k // 2, :, (k % 2) * 128 : (k % 2) * 128 + 128] = jnp.concatenate([hi, lo], axis=0)


def times_tile(x_ref, y_ref, q, i, j, tile, both):
    y_ref[q, j] += jnp.dot(x_ref[q, i], tile, preferred_element_type=F32)
    if both:
        y_ref[q, i] += lax.dot_general(
            x_ref[q, j], tile, (((1,), (1,)), ((), ())), preferred_element_type=F32
        )


def tile_place(t):
    i = t & (NB - 1)
    return i, (i + (t >> 3)) & (NB - 1)


def send_rows(y_ref, scale_ref, out_ref):
    for k in range(B // 128):
        parts = []
        for q in range(NW):
            y = y_ref[q, k // 2, :, (k % 2) * 128 : (k % 2) * 128 + 128]
            parts.append((y[0:8] + y[8:16]) * scale_ref[q : q + 1, k * 128 : k * 128 + 128])
        pair = split_pair(*(jnp.concatenate([y[s2 * SP : s2 * SP + SP] for y in parts], axis=0) for s2 in range(2)))
        for d in range(2):
            out_ref[32 * k + 16 * d : 32 * k + 16 * d + 16, :] = pair[d].astype(out_ref.dtype)


def take_vectors(first, second, k, x_ref, scale_ref):
    pair = split_pair(first, second)
    for q in range(NW):
        vec = jnp.concatenate([one[q * SP : q * SP + SP] for one in pair], axis=0)
        put_vectors(x_ref, q, k, vec * scale_ref[q : q + 1, k * 128 : k * 128 + 128])


def gen_kernel(
    r_ref, xy_ref, basis_hbm, bins_hbm, norm_hbm,
    kern_ref, amp_ref, scale_ref, psi_ref, seg_ref, norm_ref, edge_ref,
    rows_ref, la, x_ref, y_ref, sq_row, sq_col, xy_row, xy_col, dist, bins_ref, sems,
):
    copies = [
        pltpu.make_async_copy(source, target, sems.at[n])
        for n, (source, target) in enumerate(
            ((basis_hbm, psi_ref), (bins_hbm, seg_ref), (norm_hbm, norm_ref), (bins_hbm, bins_ref))
        )
    ]
    for one in copies:
        one.start()
    rows_ref[...] = r_ref[...].astype(F32)
    for k in range(B // 128):
        lanes = slice(k * 128, k * 128 + 128)
        base = 2 * k * IN_ROWS
        pair = split_pair(
            rows_ref[base + 16 : base + 24, :], rows_ref[base + IN_ROWS + 16 : base + IN_ROWS + 24, :]
        )
        for one in range(2):
            la[one, :, lanes] = pair[one]
        for c in range(2):
            row = xy_ref[c : c + 1, lanes] * ROOT
            wide = jnp.broadcast_to(row, (128, 128))
            xy_row[c, k // 2, :, (k % 2) * 128 : (k % 2) * 128 + 128] = wide[0:8]
            xy_col[c, lanes, :] = wide.T
    length = la[0, 0:NW, :] + la[0, NW : 2 * NW, :]
    amp = la[1, 0:NW, :] + la[1, NW : 2 * NW, :]
    scale_ref[NW:8, :] = jnp.zeros((8 - NW, B), F32)
    scale_ref[0:NW, :] = amp * jnp.sqrt(length * math.sqrt(2.0))
    la[0, 0:NW, :] = length * length
    for k in range(B // 128):
        lanes = slice(k * 128, k * 128 + 128)
        base = 2 * k * IN_ROWS
        take_vectors(
            rows_ref[base : base + 16, :], rows_ref[base + IN_ROWS : base + IN_ROWS + 16, :], k, x_ref, scale_ref
        )
        for q in range(NW):
            wide = jnp.broadcast_to(la[0, q : q + 1, lanes], (128, 128))
            sq_row[q, k // 2, :, (k % 2) * 128 : (k % 2) * 128 + 128] = wide[0:8]
            sq_col[q, lanes, :] = wide.T
    y_ref[...] = jnp.zeros_like(y_ref)

    step = 32

    def tile(t, both):
        i, j = tile_place(t)
        row0 = pl.multiple_of(i * TB, TB)
        for st in range(TB // step):
            rows = pl.ds(row0 + st * step, step)
            xc = xy_col[0, rows, :].reshape(step // 8, 8, 128)
            yc = xy_col[1, rows, :].reshape(step // 8, 8, 128)
            for c in range(2):
                half = slice(c * 128, c * 128 + 128)
                dx = xc - xy_row[0, j, :, half][None]
                dy = yc - xy_row[1, j, :, half][None]
                d = -(dx * dx) - dy * dy
                dist[st * step : st * step + step, half] = d.reshape(step, 128)
        for q in range(NW):
            for st in range(TB // step):
                sq = sq_col[q, pl.ds(row0 + st * step, step), :].reshape(step // 8, 8, 128)
                parts = []
                for c in range(2):
                    half = slice(c * 128, c * 128 + 128)
                    root = lax.rsqrt(sq + sq_row[q, j, :, half][None])
                    d = dist[st * step : st * step + step, half].reshape(step // 8, 8, 128)
                    parts.append((root * jnp.exp2(root * root * d)).reshape(step, 128).astype(BF16))
                kern_ref[t, q, st * step : st * step + step, :] = jnp.concatenate(parts, axis=1)
            times_tile(x_ref, y_ref, q, i, j, kern_ref[t, q], both)

    @pl.loop(0, NB)
    def _(t):
        tile(t, False)

    @pl.loop(NB, NT)
    def _(t):
        tile(t, True)

    send_rows(y_ref, scale_ref, amp_ref)
    for one in copies:
        one.wait()

    @pl.loop(0, TILES)
    def _(n):
        first = bins_ref[0, n * T]
        edge_ref[n] = first
        edge_ref[TILES + n] = bins_ref[0, n * T + T - 1] - first


def pull_kernel(g_ref, scale_ref, kern_ref, out_ref, x_ref, y_ref):
    for k in range(B // 128):
        a = g_ref[32 * k : 32 * k + 16, :].astype(F32)
        b = g_ref[32 * k + 16 : 32 * k + 32, :].astype(F32)
        take_vectors(a, b, k, x_ref, scale_ref)
    y_ref[...] = jnp.zeros_like(y_ref)

    def tile(t, both):
        i, j = tile_place(t)
        for q in range(NW):
            times_tile(x_ref, y_ref, q, i, j, kern_ref[t, q], both)

    @pl.loop(0, NB)
    def _(t):
        tile(t, False)

    @pl.loop(NB, NT)
    def _(t):
        tile(t, True)

    send_rows(y_ref, scale_ref, out_ref)


def wave_rows(ref, sp):
    return jnp.concatenate([ref[pl.ds(q * SP + sp, G, stride=16), :] for q in range(NW)], axis=0)


def forward_kernel(edge_ref, seg_ref, amp_ref, psi_ref, out0, out1, out2, out3, rows_ref, table, acc):
    me = lax.axis_index("wave")

    def tiles(k, m):
        tile = ((me + k) & (NX - 1)) * (Q // T) + m * 2
        return [(u, half, tile + half * (HQ // T) + u) for u in range(2) for half in range(2)]

    rows_ref[...] = amp_ref[...].astype(F32)
    table[...] = jnp.zeros_like(table)
    for sp in range(SP):
        flipped = wave_rows(rows_ref, sp).T
        for s2 in range(2):
            table[pl.ds(sp + SP * s2, R, stride=S), :] = flipped[s2 * R : s2 * R + R]

    for k, out_ref in enumerate((out0, out1, out2, out3)):

        @pl.loop(0, 4)
        def _(m):
            places = tiles(k, m)

            def select(u, half, tile, first, start):
                window = table[pl.ds(pl.multiple_of(first * S, S), NWIN * S), :].astype(BF16)
                values = psi_ref[pl.ds(pl.multiple_of(tile * T, T), T), :]
                fields = lax.dot_general(
                    window, values, (((1,), (1,)), ((), ())), preferred_element_type=F32
                )
                seg = jnp.broadcast_to(seg_ref[0:1, pl.ds(pl.multiple_of(tile * T, T), T)], (S, T)) - first
                for g in range(NWIN):
                    start = jnp.where(seg == g, fields[g * S : g * S + S], start)
                return start

            spans = []
            for u, half, tile in places:
                first = edge_ref[tile]
                acc[u, half * S : half * S + S, :] = select(u, half, tile, first, jnp.zeros((S, T), F32))
                spans.append(edge_ref[TILES + tile])
            widest = jnp.maximum(jnp.maximum(spans[0], spans[1]), jnp.maximum(spans[2], spans[3]))

            @pl.when(widest >= NWIN)
            def _():
                for (u, half, tile), span in zip(places, spans):
                    first = edge_ref[tile]

                    @pl.loop(1, span // NWIN + 1)
                    def _(w):
                        old = acc[u, half * S : half * S + S, :]
                        acc[u, half * S : half * S + S, :] = select(u, half, tile, first + w * NWIN, old)

            for u in range(2):
                out_ref[:, pl.ds(pl.multiple_of(m * 1024 + u * T, T), T)] = acc[u].astype(BF16)


def weight_kernel(a_ref, b_ref, c_ref, d_ref, out_ref):
    field = (a_ref[...].astype(F32) + b_ref[...].astype(F32)) + (c_ref[...].astype(F32) + d_ref[...].astype(F32))
    out_ref[...] = (-2.0 / S * field / (1.0 + field * field)).astype(BF16)


def backward_kernel(edge_ref, w0_ref, w1_ref, w2_ref, w3_ref, seg_ref, amp_ref, norm_ref, psi_ref, out_ref, rows_ref, sums):
    me = lax.axis_index("wave")

    def tiles(k, m):
        tile = ((me - k) & (NX - 1)) * (Q // T) + m * 2
        return [(u, half, tile + half * (HQ // T) + u) for u in range(2) for half in range(2)]

    sums[...] = jnp.zeros_like(sums)
    for k, w_ref in enumerate((w0_ref, w1_ref, w2_ref, w3_ref)):

        @pl.loop(0, 4)
        def _(m):
            places = tiles(k, m)

            def add(u, half, tile, first):
                weight = w_ref[:, pl.ds(pl.multiple_of(m * 1024 + u * T, T), T)].astype(F32)
                weight = weight[half * S : half * S + S]
                values = psi_ref[pl.ds(pl.multiple_of(tile * T, T), T), :]
                seg = jnp.broadcast_to(seg_ref[0:1, pl.ds(pl.multiple_of(tile * T, T), T)], (S, T)) - first
                spread = jnp.concatenate([jnp.where(seg == g, weight, 0.0) for g in range(NWIN)], axis=0)
                added = jnp.dot(spread.astype(BF16), values, preferred_element_type=F32)
                sums[pl.ds(pl.multiple_of(first * S, S), NWIN * S), :] += added

            spans = []
            for u, half, tile in places:
                first = edge_ref[tile]
                add(u, half, tile, first)
                spans.append(edge_ref[TILES + tile])
            widest = jnp.maximum(jnp.maximum(spans[0], spans[1]), jnp.maximum(spans[2], spans[3]))

            @pl.when(widest >= NWIN)
            def _():
                for (u, half, tile), span in zip(places, spans):
                    first = edge_ref[tile]

                    @pl.loop(1, span // NWIN + 1)
                    def _(w):
                        add(u, half, tile, first + w * NWIN)

    rows_ref[...] = amp_ref[...].astype(F32)
    norm = (jnp.concatenate([norm_ref[...]] * 2, axis=0) * (2.0 / S)).T
    for sp in range(SP):
        pair = [sums[pl.ds(sp + SP * s2, R, stride=S), :] for s2 in range(2)]
        flipped = jnp.concatenate(pair, axis=0).T
        for q in range(NW):
            where = pl.ds(q * SP + sp, G, stride=16)
            rows_ref[where, :] = rows_ref[where, :] * norm[q * G : q * G + G] + flipped[q * G : q * G + G]
    out_ref[...] = rows_ref[...].astype(BF16)


def unpack_kernel(r_ref, lat_ref, out_ref):
    for sp in range(SP):
        flipped = wave_rows(r_ref, sp).T
        for s2 in range(2):
            s = sp + SP * s2
            out_ref[s] = flipped[s2 * R : s2 * R + R] + lat_ref[s].astype(F32)


def exchange(x, rows):
    y = lax.all_to_all(x.reshape(G, rows, 128), "event", 0, 0)
    return y.reshape(G * rows, 128)


def shift(x, k):
    return lax.ppermute(x, "wave", [(i, (i + k) % NX) for i in range(NX)])


def vmem(shape, dtype=BF16):
    return pltpu.VMEM(shape, dtype)


def call(kernel, name, out_shape, args, scratch=(), spaces=None, out_specs=None, mib=8):
    spaces = spaces or "v" * len(args)
    kept = {"v": pltpu.VMEM, "h": pltpu.HBM}
    args = [pltpu.with_memory_space_constraint(a, kept[c]) if c in kept else a for a, c in zip(args, spaces)]
    return pl.pallas_call(
        kernel,
        out_shape=out_shape,
        in_specs=[{"v": VMEM, "h": ANY, "s": SMEM}[c] for c in spaces],
        out_specs=out_specs or jax.tree.map(lambda _: VMEM, out_shape),
        scratch_shapes=scratch,
        compiler_params=pltpu.CompilerParams(vmem_limit_bytes=mib * 1024 * 1024),
        name=name,
    )(*args)


def shards(latent, basis, event_bin, length, amplitude_scale, yield_norm, bin_coords):
    latent = latent.transpose(0, 2, 1)
    packed, coords, lat_kept = call(
        pack_kernel,
        "pack",
        (vmem((G * IN_ROWS, 128)), vmem((2, B), F32), vmem((S, R, WL))),
        (latent, length.T, amplitude_scale.T, bin_coords),
        [
            vmem((R, WL), F32),
            vmem((R, WL), F32),
            vmem((G * IN_ROWS, 128), F32),
            pltpu.SemaphoreType.DMA((4,)),
        ],
        "hhhh",
    )
    kern, amp_out, scale, psi, seg, norm, edges = call(
        gen_kernel,
        "gen",
        (
            vmem((NT, NW, TB, TB)),
            vmem((G * 16, 128)),
            vmem((8, B), F32),
            vmem((E, WL)),
            vmem((1, E), jnp.int32),
            vmem((R, WL), F32),
            jax.ShapeDtypeStruct((2 * TILES,), jnp.int32),
        ),
        (exchange(packed, IN_ROWS), coords, basis, event_bin, yield_norm.T),
        [
            vmem((G * IN_ROWS, 128), F32),
            vmem((2, 8, B), F32),
            vmem((NW, NB, 16, TB)),
            vmem((NW, NB, 16, TB), F32),
            vmem((NW, NB, 8, TB), F32),
            vmem((NW, B, 128), F32),
            vmem((2, NB, 8, TB), F32),
            vmem((2, B, 128), F32),
            vmem((TB, TB), F32),
            pltpu.SMEM((1, E), jnp.int32),
            pltpu.SemaphoreType.DMA((4,)),
        ],
        "vvhhh",
        (VMEM,) * 6 + (SMEM,),
        mib=12,
    )
    amp_in = exchange(amp_out, 16)
    fields = call(
        forward_kernel,
        "forward",
        [vmem((2 * S, HQ))] * NX,
        (edges, seg, amp_in, psi),
        [
            vmem((G * 16, 128), F32),
            vmem(((R + NWIN) * S, 128), F32),
            vmem((2, 2 * S, T), F32),
        ],
        "svvv",
    )
    others = [shift(fields[k], k) for k in range(1, NX)]
    weight = call(weight_kernel, "weight", vmem((2 * S, HQ)), (fields[0], *others))
    weights = [weight] + [shift(weight, k) for k in range(1, NX)]
    grad_out = call(
        backward_kernel,
        "backward",
        vmem((G * 16, 128)),
        (edges, *weights, seg, amp_in, norm, psi),
        [vmem((G * 16, 128), F32), vmem(((R + NWIN) * S, 128), F32)],
        "svvvvvvvv",
    )
    pulled = call(
        pull_kernel,
        "pull",
        vmem((G * 16, 128), F32),
        (exchange(grad_out, 16), scale, kern),
        [vmem((NW, NB, 16, TB)), vmem((NW, NB, 16, TB), F32)],
    )
    out = call(
        unpack_kernel,
        "unpack",
        jax.ShapeDtypeStruct((S, R, WL), F32),
        (exchange(pulled, 16), lat_kept),
    )
    return out.transpose(0, 2, 1)


def solution(mesh):
    placed = (
        P(None, "wave", "event"),
        P("event", "wave"),
        P("event", None),
        P("wave", "event"),
        P("wave", "event"),
        P("wave", "event"),
        P(),
    )
    return jax.shard_map(
        shards, mesh=mesh, in_specs=placed, out_specs=P(None, "wave", "event"), check_vma=False
    )
```

```python
import functools
import math

import jax
import jax.numpy as jnp
from jax import lax
from jax.experimental import pallas as pl
from jax.experimental.pallas import tpu as pltpu
from jax.sharding import PartitionSpec as P

F32 = jnp.float32
BF16 = jnp.bfloat16

S, WL, R, B, E, G, NW = 8, 128, 64, 2048, 32768, 32, 4
NX = 4
SP = 4
TB = 256
NB = B // TB
NT = NB + NB * (NB - 1) // 2
IN_ROWS = 24
T = 512
TILES = E // T
Q = E // NX
HQ = Q // 2
NWIN = 8
ROOT = math.sqrt(math.log2(math.e))
VMEM = pl.BlockSpec(memory_space=pltpu.VMEM)
SMEM = pl.BlockSpec(memory_space=pltpu.SMEM)
ANY = pl.BlockSpec(memory_space=pl.ANY)


def low_lanes(shape):
    return lax.broadcasted_iota(jnp.int32, shape, len(shape) - 1) < 64


def swap(x):
    return pltpu.roll(x, 64, 1)


def pack_kernel(lat_hbm, len_hbm, amp_hbm, xy_hbm, out_ref, xy_ref, lat_ref, len_ref, amp_ref, rows, sems):
    copies = [
        pltpu.make_async_copy(source, target, sems.at[n])
        for n, (source, target) in enumerate(
            ((lat_hbm, lat_ref), (len_hbm, len_ref), (amp_hbm, amp_ref), (xy_hbm, xy_ref))
        )
    ]
    for one in copies:
        one.start()

    def put(row, value):
        for q in range(NW):
            rows[pl.ds(row(q), G, stride=IN_ROWS), :] = value[q * G : q * G + G]

    copies[0].wait()
    for sp in range(SP):
        pair = jnp.concatenate([lat_ref[sp], lat_ref[sp + SP]], axis=0).astype(F32)
        put(lambda q: q * SP + sp, pair.T)
    copies[1].wait()
    copies[2].wait()
    exact = jnp.concatenate([len_ref[...], amp_ref[...]], axis=0).T
    high = exact.astype(BF16).astype(F32)
    put(lambda q: 16 + q, high)
    put(lambda q: 20 + q, exact - high)
    out_ref[...] = rows[...].astype(BF16)
    copies[3].wait()


def split_pair(a, b):
    low = low_lanes(a.shape)
    return jnp.where(low, a, swap(b)), jnp.where(low, swap(a), b)


def put_vectors(x_ref, q, k, vec):
    hi = vec.astype(BF16)
    lo = (vec - hi.astype(F32)).astype(BF16)
    x_ref[q, k // 2, :, (k % 2) * 128 : (k % 2) * 128 + 128] = jnp.concatenate([hi, lo], axis=0)


def times_tile(x_ref, y_ref, q, i, j, tile, both):
    y_ref[q, j] += jnp.dot(x_ref[q, i], tile, preferred_element_type=F32)
    if both:
        y_ref[q, i] += lax.dot_general(
            x_ref[q, j], tile, (((1,), (1,)), ((), ())), preferred_element_type=F32
        )


def tile_place(t):
    i = t & (NB - 1)
    return i, (i + (t >> 3)) & (NB - 1)


def send_rows(y_ref, scale_ref, out_ref):
    for k in range(B // 128):
        parts = []
        for q in range(NW):
            y = y_ref[q, k // 2, :, (k % 2) * 128 : (k % 2) * 128 + 128]
            parts.append((y[0:8] + y[8:16]) * scale_ref[q : q + 1, k * 128 : k * 128 + 128])
        pair = split_pair(*(jnp.concatenate([y[s2 * SP : s2 * SP + SP] for y in parts], axis=0) for s2 in range(2)))
        for d in range(2):
            out_ref[32 * k + 16 * d : 32 * k + 16 * d + 16, :] = pair[d].astype(out_ref.dtype)


def take_vectors(first, second, k, x_ref, scale_ref):
    pair = split_pair(first, second)
    for q in range(NW):
        vec = jnp.concatenate([one[q * SP : q * SP + SP] for one in pair], axis=0)
        put_vectors(x_ref, q, k, vec * scale_ref[q : q + 1, k * 128 : k * 128 + 128])


def gen_kernel(
    r_ref, xy_ref, basis_hbm, bins_hbm, norm_hbm,
    kern_ref, amp_ref, scale_ref, psi_ref, seg_ref, norm_ref, edge_ref,
    rows_ref, la, x_ref, y_ref, sq_row, sq_col, xy_row, xy_col, dist, bins_ref, sems,
):
    copies = [
        pltpu.make_async_copy(source, target, sems.at[n])
        for n, (source, target) in enumerate(
            ((basis_hbm, psi_ref), (bins_hbm, seg_ref), (norm_hbm, norm_ref), (bins_hbm, bins_ref))
        )
    ]
    for one in copies:
        one.start()
    rows_ref[...] = r_ref[...].astype(F32)
    for k in range(B // 128):
        lanes = slice(k * 128, k * 128 + 128)
        base = 2 * k * IN_ROWS
        pair = split_pair(
            rows_ref[base + 16 : base + 24, :], rows_ref[base + IN_ROWS + 16 : base + IN_ROWS + 24, :]
        )
        for one in range(2):
            la[one, :, lanes] = pair[one]
        for c in range(2):
            row = xy_ref[c : c + 1, lanes] * ROOT
            wide = jnp.broadcast_to(row, (128, 128))
            xy_row[c, k // 2, :, (k % 2) * 128 : (k % 2) * 128 + 128] = wide[0:8]
            xy_col[c, lanes, :] = wide.T
    length = la[0, 0:NW, :] + la[0, NW : 2 * NW, :]
    amp = la[1, 0:NW, :] + la[1, NW : 2 * NW, :]
    scale_ref[NW:8, :] = jnp.zeros((8 - NW, B), F32)
    scale_ref[0:NW, :] = amp * jnp.sqrt(length * math.sqrt(2.0))
    la[0, 0:NW, :] = length * length
    for k in range(B // 128):
        lanes = slice(k * 128, k * 128 + 128)
        base = 2 * k * IN_ROWS
        take_vectors(
            rows_ref[base : base + 16, :], rows_ref[base + IN_ROWS : base + IN_ROWS + 16, :], k, x_ref, scale_ref
        )
        for q in range(NW):
            wide = jnp.broadcast_to(la[0, q : q + 1, lanes], (128, 128))
            sq_row[q, k // 2, :, (k % 2) * 128 : (k % 2) * 128 + 128] = wide[0:8]
            sq_col[q, lanes, :] = wide.T
    y_ref[...] = jnp.zeros_like(y_ref)

    step = 32

    def tile(t, both):
        i, j = tile_place(t)
        row0 = pl.multiple_of(i * TB, TB)
        for st in range(TB // step):
            rows = pl.ds(row0 + st * step, step)
            xc = xy_col[0, rows, :].reshape(step // 8, 8, 128)
            yc = xy_col[1, rows, :].reshape(step // 8, 8, 128)
            for c in range(2):
                half = slice(c * 128, c * 128 + 128)
                dx = xc - xy_row[0, j, :, half][None]
                dy = yc - xy_row[1, j, :, half][None]
                d = -(dx * dx) - dy * dy
                dist[st * step : st * step + step, half] = d.reshape(step, 128)
        for q in range(NW):
            for st in range(TB // step):
                sq = sq_col[q, pl.ds(row0 + st * step, step), :].reshape(step // 8, 8, 128)
                parts = []
                for c in range(2):
                    half = slice(c * 128, c * 128 + 128)
                    root = lax.rsqrt(sq + sq_row[q, j, :, half][None])
                    d = dist[st * step : st * step + step, half].reshape(step // 8, 8, 128)
                    parts.append((root * jnp.exp2(root * root * d)).reshape(step, 128).astype(BF16))
                kern_ref[t, q, st * step : st * step + step, :] = jnp.concatenate(parts, axis=1)
            times_tile(x_ref, y_ref, q, i, j, kern_ref[t, q], both)

    @pl.loop(0, NB, unroll=8)
    def _(t):
        tile(t, False)

    @pl.loop(NB, NT, unroll=7)
    def _(t):
        tile(t, True)

    send_rows(y_ref, scale_ref, amp_ref)
    for one in copies:
        one.wait()

    for quarter in range(NX):
        widest = jnp.int32(0)
        for n in range(quarter * TILES // NX, (quarter + 1) * TILES // NX):
            first = bins_ref[0, n * T]
            span = bins_ref[0, n * T + T - 1] - first
            edge_ref[n] = first
            edge_ref[TILES + n] = span
            widest = jnp.maximum(widest, span)
        edge_ref[2 * TILES + quarter] = widest


def pull_kernel(g_ref, scale_ref, kern_ref, out_ref, x_ref, y_ref):
    for k in range(B // 128):
        a = g_ref[32 * k : 32 * k + 16, :].astype(F32)
        b = g_ref[32 * k + 16 : 32 * k + 32, :].astype(F32)
        take_vectors(a, b, k, x_ref, scale_ref)
    y_ref[...] = jnp.zeros_like(y_ref)

    def tile(t, both):
        i, j = tile_place(t)
        for q in range(NW):
            times_tile(x_ref, y_ref, q, i, j, kern_ref[t, q], both)

    @pl.loop(0, NB, unroll=8)
    def _(t):
        tile(t, False)

    @pl.loop(NB, NT, unroll=7)
    def _(t):
        tile(t, True)

    send_rows(y_ref, scale_ref, out_ref)


def wave_rows(ref, sp):
    return jnp.concatenate([ref[pl.ds(q * SP + sp, G, stride=16), :] for q in range(NW)], axis=0)


def table_kernel(amp_ref, table_ref, rows_ref):
    rows_ref[...] = amp_ref[...].astype(F32)
    table_ref[R * S :, :] = jnp.zeros((NWIN * S, WL), F32)
    for sp in range(SP):
        flipped = wave_rows(rows_ref, sp).T
        for s2 in range(2):
            table_ref[pl.ds(sp + SP * s2, R, stride=S), :] = flipped[s2 * R : s2 * R + R]


def quarter_tiles(quarter, m):
    tile = quarter * (Q // T) + m
    return tile, tile + HQ // T


def tile_bins(seg_ref, tile, first):
    return jnp.broadcast_to(seg_ref[0:1, pl.ds(pl.multiple_of(tile * T, T), T)], (S, T)) - first


def tile_basis(psi_ref, tile):
    return psi_ref[pl.ds(pl.multiple_of(tile * T, T), T), :]


def forward_kernel(k, edge_ref, seg_ref, table_ref, psi_ref, out_ref):
    quarter = (lax.axis_index("wave") + k) & (NX - 1)

    def select(tile, first, start):
        window = table_ref[pl.ds(pl.multiple_of(first * S, S), NWIN * S), :].astype(BF16)
        fields = lax.dot_general(
            window, tile_basis(psi_ref, tile), (((1,), (1,)), ((), ())), preferred_element_type=F32
        )
        seg = tile_bins(seg_ref, tile, first)
        for g in range(NWIN):
            start = jnp.where(seg == g, fields[g * S : g * S + S], start)
        return start

    def put(m, parts):
        out_ref[:, pl.ds(pl.multiple_of(m * T, T), T)] = jnp.concatenate(parts, axis=0).astype(BF16)

    zero = jnp.zeros((S, T), F32)

    for m in range(HQ // T):
        put(m, [select(tile, edge_ref[tile], zero) for tile in quarter_tiles(quarter, m)])

    @pl.when(edge_ref[2 * TILES + quarter] >= NWIN)
    def _():
        @pl.loop(0, HQ // T)
        def _(m):
            put(
                m,
                [
                    lax.fori_loop(
                        0,
                        edge_ref[TILES + tile] // NWIN + 1,
                        lambda w, acc: select(tile, edge_ref[tile] + w * NWIN, acc),
                        zero,
                    )
                    for tile in quarter_tiles(quarter, m)
                ],
            )


def weight_kernel(a_ref, b_ref, c_ref, d_ref, out_ref):
    field = (a_ref[...].astype(F32) + b_ref[...].astype(F32)) + (c_ref[...].astype(F32) + d_ref[...].astype(F32))
    out_ref[...] = (-2.0 / S * field / (1.0 + field * field)).astype(BF16)


def add_quarter(k, edge_ref, w_ref, seg_ref, psi_ref, sums):
    quarter = (lax.axis_index("wave") - k) & (NX - 1)

    def add(m, half, tile, first):
        weight = w_ref[:, pl.ds(pl.multiple_of(m * T, T), T)].astype(F32)[half * S : half * S + S]
        seg = tile_bins(seg_ref, tile, first)
        spread = jnp.concatenate([jnp.where(seg == g, weight, 0.0) for g in range(NWIN)], axis=0)
        added = jnp.dot(spread.astype(BF16), tile_basis(psi_ref, tile), preferred_element_type=F32)
        sums[pl.ds(pl.multiple_of(first * S, S), NWIN * S), :] += added

    for m in range(HQ // T):
        for half, tile in enumerate(quarter_tiles(quarter, m)):
            add(m, half, tile, edge_ref[tile])

    @pl.when(edge_ref[2 * TILES + quarter] >= NWIN)
    def _():
        @pl.loop(0, HQ // T)
        def _(m):
            for half, tile in enumerate(quarter_tiles(quarter, m)):

                @pl.loop(1, edge_ref[TILES + tile] // NWIN + 1)
                def _(w):
                    add(m, half, tile, edge_ref[tile] + w * NWIN)


def backward_first_kernel(edge_ref, w0_ref, seg_ref, psi_ref, sums_ref):
    sums_ref[...] = jnp.zeros_like(sums_ref)
    add_quarter(0, edge_ref, w0_ref, seg_ref, psi_ref, sums_ref)


def backward_kernel(edge_ref, w1_ref, w2_ref, w3_ref, seg_ref, psi_ref, begun_ref, amp_ref, norm_ref, out_ref, rows_ref, sums):
    sums[...] = begun_ref[...]
    for k, w_ref in enumerate((w1_ref, w2_ref, w3_ref)):
        add_quarter(k + 1, edge_ref, w_ref, seg_ref, psi_ref, sums)
    rows_ref[...] = amp_ref[...].astype(F32)
    norm = (jnp.concatenate([norm_ref[...]] * 2, axis=0) * (2.0 / S)).T
    for sp in range(SP):
        pair = [sums[pl.ds(sp + SP * s2, R, stride=S), :] for s2 in range(2)]
        flipped = jnp.concatenate(pair, axis=0).T
        for q in range(NW):
            where = pl.ds(q * SP + sp, G, stride=16)
            rows_ref[where, :] = rows_ref[where, :] * norm[q * G : q * G + G] + flipped[q * G : q * G + G]
    out_ref[...] = rows_ref[...].astype(BF16)


def unpack_kernel(r_ref, lat_ref, out_ref):
    for sp in range(SP):
        flipped = wave_rows(r_ref, sp).T
        for s2 in range(2):
            s = sp + SP * s2
            out_ref[s] = flipped[s2 * R : s2 * R + R] + lat_ref[s].astype(F32)


def exchange(x, rows):
    y = lax.all_to_all(x.reshape(G, rows, 128), "event", 0, 0)
    return y.reshape(G * rows, 128)


def shift(x, k):
    return lax.ppermute(x, "wave", [(i, (i + k) % NX) for i in range(NX)])


def vmem(shape, dtype=BF16):
    return pltpu.VMEM(shape, dtype)


def call(kernel, name, out_shape, args, scratch=(), spaces=None, out_specs=None, mib=8):
    spaces = spaces or "v" * len(args)
    kept = {"v": pltpu.VMEM, "h": pltpu.HBM}
    args = [pltpu.with_memory_space_constraint(a, kept[c]) if c in kept else a for a, c in zip(args, spaces)]
    return pl.pallas_call(
        kernel,
        out_shape=out_shape,
        in_specs=[{"v": VMEM, "h": ANY, "s": SMEM}[c] for c in spaces],
        out_specs=out_specs or jax.tree.map(lambda _: VMEM, out_shape),
        scratch_shapes=scratch,
        compiler_params=pltpu.CompilerParams(vmem_limit_bytes=mib * 1024 * 1024),
        name=name,
    )(*args)


def shards(latent, basis, event_bin, length, amplitude_scale, yield_norm, bin_coords):
    latent = latent.transpose(0, 2, 1)
    packed, coords, lat_kept = call(
        pack_kernel,
        "pack",
        (vmem((G * IN_ROWS, 128)), vmem((2, B), F32), vmem((S, R, WL))),
        (latent, length.T, amplitude_scale.T, bin_coords),
        [
            vmem((R, WL), F32),
            vmem((R, WL), F32),
            vmem((G * IN_ROWS, 128), F32),
            pltpu.SemaphoreType.DMA((4,)),
        ],
        "hhhh",
    )
    kern, amp_out, scale, psi, seg, norm, edges = call(
        gen_kernel,
        "gen",
        (
            vmem((NT, NW, TB, TB)),
            vmem((G * 16, 128)),
            vmem((8, B), F32),
            vmem((E, WL)),
            vmem((1, E), jnp.int32),
            vmem((R, WL), F32),
            jax.ShapeDtypeStruct((2 * TILES + NX,), jnp.int32),
        ),
        (exchange(packed, IN_ROWS), coords, basis, event_bin, yield_norm.T),
        [
            vmem((G * IN_ROWS, 128), F32),
            vmem((2, 8, B), F32),
            vmem((NW, NB, 16, TB)),
            vmem((NW, NB, 16, TB), F32),
            vmem((NW, NB, 8, TB), F32),
            vmem((NW, B, 128), F32),
            vmem((2, NB, 8, TB), F32),
            vmem((2, B, 128), F32),
            vmem((TB, TB), F32),
            pltpu.SMEM((1, E), jnp.int32),
            pltpu.SemaphoreType.DMA((4,)),
        ],
        "vvhhh",
        (VMEM,) * 6 + (SMEM,),
        mib=12,
    )
    amp_in = exchange(amp_out, 16)
    bins = (R + NWIN) * S
    table = call(table_kernel, "table", vmem((bins, WL), F32), (amp_in,), [vmem((G * 16, 128), F32)])

    def forward(k):
        return call(
            functools.partial(forward_kernel, k), "forward", vmem((2 * S, HQ)), (edges, seg, table, psi), spaces="svvv"
        )

    others = [shift(forward(k), k) for k in (2, 1, 3)]
    weight = call(weight_kernel, "weight", vmem((2 * S, HQ)), (forward(0), *others))
    weights = [shift(weight, k) for k in range(1, NX)]
    begun = call(
        backward_first_kernel, "backward0", vmem((bins, WL), F32), (edges, weight, seg, psi), spaces="svvv"
    )
    grad_out = call(
        backward_kernel,
        "backward",
        vmem((G * 16, 128)),
        (edges, *weights, seg, psi, begun, amp_in, norm),
        [vmem((G * 16, 128), F32), vmem((bins, WL), F32)],
        "svvvvvvvv",
    )
    pulled = call(
        pull_kernel,
        "pull",
        vmem((G * 16, 128), F32),
        (exchange(grad_out, 16), scale, kern),
        [vmem((NW, NB, 16, TB)), vmem((NW, NB, 16, TB), F32)],
    )
    out = call(
        unpack_kernel,
        "unpack",
        jax.ShapeDtypeStruct((S, R, WL), F32),
        (exchange(pulled, 16), lat_kept),
    )
    return out.transpose(0, 2, 1)


def solution(mesh):
    placed = (
        P(None, "wave", "event"),
        P("event", "wave"),
        P("event", None),
        P("wave", "event"),
        P("wave", "event"),
        P("wave", "event"),
        P(),
    )
    return jax.shard_map(
        shards, mesh=mesh, in_specs=placed, out_specs=P(None, "wave", "event"), check_vma=False
    )
```

```python
import functools
import math

import jax
import jax.numpy as jnp
from jax import lax
from jax.experimental import pallas as pl
from jax.experimental.pallas import tpu as pltpu
from jax.sharding import PartitionSpec as P

F32 = jnp.float32
BF16 = jnp.bfloat16

S, WL, R, B, E, G, NW = 8, 128, 64, 2048, 32768, 32, 4
NX = 4
SP = 4
TB = 256
NB = B // TB
NT = NB + NB * (NB - 1) // 2
IN_ROWS = 24
T = 512
TILES = E // T
COST = 10**9
Q = E // NX
HQ = Q // 2
NWIN = 8
ROOT = math.sqrt(math.log2(math.e))
VMEM = pl.BlockSpec(memory_space=pltpu.VMEM)
SMEM = pl.BlockSpec(memory_space=pltpu.SMEM)
ANY = pl.BlockSpec(memory_space=pl.ANY)


def low_lanes(shape):
    return lax.broadcasted_iota(jnp.int32, shape, len(shape) - 1) < 64


def swap(x):
    return pltpu.roll(x, 64, 1)


def pack_kernel(lat_hbm, len_hbm, amp_hbm, xy_hbm, out_ref, xy_ref, lat_ref, len_ref, amp_ref, rows, sems):
    copies = [
        pltpu.make_async_copy(source, target, sems.at[n])
        for n, (source, target) in enumerate(
            ((lat_hbm, lat_ref), (len_hbm, len_ref), (amp_hbm, amp_ref), (xy_hbm, xy_ref))
        )
    ]
    for one in copies:
        one.start()

    def put(row, value):
        for q in range(NW):
            rows[pl.ds(row(q), G, stride=IN_ROWS), :] = value[q * G : q * G + G]

    copies[0].wait()
    for sp in range(SP):
        pair = jnp.concatenate([lat_ref[sp], lat_ref[sp + SP]], axis=0).astype(F32)
        put(lambda q: q * SP + sp, pair.T)
    copies[1].wait()
    copies[2].wait()
    exact = jnp.concatenate([len_ref[...], amp_ref[...]], axis=0).T
    high = exact.astype(BF16).astype(F32)
    put(lambda q: 16 + q, high)
    put(lambda q: 20 + q, exact - high)
    out_ref[...] = rows[...].astype(BF16)
    copies[3].wait()


def split_pair(a, b):
    low = low_lanes(a.shape)
    return jnp.where(low, a, swap(b)), jnp.where(low, swap(a), b)


def put_vectors(x_ref, q, k, vec):
    hi = vec.astype(BF16)
    lo = (vec - hi.astype(F32)).astype(BF16)
    x_ref[q, k // 2, :, (k % 2) * 128 : (k % 2) * 128 + 128] = jnp.concatenate([hi, lo], axis=0)


def times_tile(x_ref, y_ref, q, i, j, tile, both):
    y_ref[q, j] += jnp.dot(x_ref[q, i], tile, preferred_element_type=F32)
    if both:
        y_ref[q, i] += lax.dot_general(
            x_ref[q, j], tile, (((1,), (1,)), ((), ())), preferred_element_type=F32
        )


def tile_place(t):
    i = t & (NB - 1)
    return i, (i + (t >> 3)) & (NB - 1)


def send_rows(y_ref, scale_ref, out_ref):
    for k in range(B // 128):
        parts = []
        for q in range(NW):
            y = y_ref[q, k // 2, :, (k % 2) * 128 : (k % 2) * 128 + 128]
            parts.append((y[0:8] + y[8:16]) * scale_ref[q : q + 1, k * 128 : k * 128 + 128])
        pair = split_pair(*(jnp.concatenate([y[s2 * SP : s2 * SP + SP] for y in parts], axis=0) for s2 in range(2)))
        for d in range(2):
            out_ref[32 * k + 16 * d : 32 * k + 16 * d + 16, :] = pair[d].astype(out_ref.dtype)


def take_vectors(first, second, k, x_ref, scale_ref):
    pair = split_pair(first, second)
    for q in range(NW):
        vec = jnp.concatenate([one[q * SP : q * SP + SP] for one in pair], axis=0)
        put_vectors(x_ref, q, k, vec * scale_ref[q : q + 1, k * 128 : k * 128 + 128])


def gen_kernel(
    r_ref, xy_ref, basis_hbm, bins_hbm, norm_hbm,
    kern_ref, amp_ref, scale_ref, psi_ref, seg_ref, norm_ref, edge_ref,
    rows_ref, la, x_ref, y_ref, sq_row, sq_col, xy_row, xy_col, bins_ref, sems,
):
    copies = [
        pltpu.make_async_copy(source, target, sems.at[n])
        for n, (source, target) in enumerate(
            ((basis_hbm, psi_ref), (bins_hbm, seg_ref), (norm_hbm, norm_ref), (bins_hbm, bins_ref))
        )
    ]
    for one in copies:
        one.start()
    rows_ref[...] = r_ref[...].astype(F32)
    for k in range(B // 128):
        lanes = slice(k * 128, k * 128 + 128)
        base = 2 * k * IN_ROWS
        pair = split_pair(
            rows_ref[base + 16 : base + 24, :], rows_ref[base + IN_ROWS + 16 : base + IN_ROWS + 24, :]
        )
        for one in range(2):
            la[one, :, lanes] = pair[one]
        for c in range(2):
            row = xy_ref[c : c + 1, lanes] * ROOT
            wide = jnp.broadcast_to(row, (128, 128))
            xy_row[c, k // 2, :, (k % 2) * 128 : (k % 2) * 128 + 128] = wide[0:8]
            xy_col[c, lanes, :] = wide.T
    length = la[0, 0:NW, :] + la[0, NW : 2 * NW, :]
    amp = la[1, 0:NW, :] + la[1, NW : 2 * NW, :]
    scale_ref[NW:8, :] = jnp.zeros((8 - NW, B), F32)
    scale_ref[0:NW, :] = amp * jnp.sqrt(length * math.sqrt(2.0))
    la[0, 0:NW, :] = length * length
    for k in range(B // 128):
        lanes = slice(k * 128, k * 128 + 128)
        base = 2 * k * IN_ROWS
        take_vectors(
            rows_ref[base : base + 16, :], rows_ref[base + IN_ROWS : base + IN_ROWS + 16, :], k, x_ref, scale_ref
        )
        for q in range(NW):
            wide = jnp.broadcast_to(la[0, q : q + 1, lanes], (128, 128))
            sq_row[q, k // 2, :, (k % 2) * 128 : (k % 2) * 128 + 128] = wide[0:8]
            sq_col[q, lanes, :] = wide.T
    y_ref[...] = jnp.zeros_like(y_ref)

    step = 32

    def tile(t, both):
        i, j = tile_place(t)
        row0 = pl.multiple_of(i * TB, TB)
        for st in range(TB // step):
            rows = pl.ds(row0 + st * step, step)
            xc = xy_col[0, rows, :].reshape(step // 8, 8, 128)
            yc = xy_col[1, rows, :].reshape(step // 8, 8, 128)
            near = []
            for c in range(2):
                half = slice(c * 128, c * 128 + 128)
                dx = xc - xy_row[0, j, :, half][None]
                dy = yc - xy_row[1, j, :, half][None]
                near.append(-(dx * dx) - dy * dy)
            made = range(2) if both or 2 * st * step < TB else range(1, 2)
            for q in range(NW):
                sq = sq_col[q, rows, :].reshape(step // 8, 8, 128)
                parts = []
                for c in made:
                    root = lax.rsqrt(sq + sq_row[q, j, :, c * 128 : c * 128 + 128][None])
                    parts.append((root * jnp.exp2(root * root * near[c])).reshape(step, 128).astype(BF16))
                kern_ref[t, q, st * step : st * step + step, made[0] * 128 :] = jnp.concatenate(parts, axis=1)
        if not both:
            for q in range(NW):
                kern_ref[t, q, 128:, 0:128] = kern_ref[t, q, 0:128, 128:].T
        for q in range(NW):
            times_tile(x_ref, y_ref, q, i, j, kern_ref[t, q], both)

    @pl.loop(0, NB, unroll=8)
    def _(t):
        tile(t, False)

    @pl.loop(NB, NT, unroll=7)
    def _(t):
        tile(t, True)

    send_rows(y_ref, scale_ref, amp_ref)
    for one in copies:
        one.wait()

    for quarter in range(NX):
        widest = jnp.int32(0)
        for n in range(quarter * TILES // NX, (quarter + 1) * TILES // NX):
            first = bins_ref[0, n * T]
            span = bins_ref[0, n * T + T - 1] - first
            edge_ref[n] = first
            edge_ref[TILES + n] = span
            widest = jnp.maximum(widest, span)
        edge_ref[2 * TILES + quarter] = widest


def pull_kernel(g_ref, scale_ref, kern_ref, out_ref, x_ref, y_ref):
    for k in range(B // 128):
        a = g_ref[32 * k : 32 * k + 16, :].astype(F32)
        b = g_ref[32 * k + 16 : 32 * k + 32, :].astype(F32)
        take_vectors(a, b, k, x_ref, scale_ref)
    y_ref[...] = jnp.zeros_like(y_ref)

    def tile(t, both):
        i, j = tile_place(t)
        for q in range(NW):
            times_tile(x_ref, y_ref, q, i, j, kern_ref[t, q], both)

    @pl.loop(0, NB, unroll=8)
    def _(t):
        tile(t, False)

    @pl.loop(NB, NT, unroll=28)
    def _(t):
        tile(t, True)

    send_rows(y_ref, scale_ref, out_ref)


def wave_rows(ref, sp):
    return jnp.concatenate([ref[pl.ds(q * SP + sp, G, stride=16), :] for q in range(NW)], axis=0)


def table_kernel(amp_ref, table_ref, rows_ref):
    rows_ref[...] = amp_ref[...].astype(F32)
    table_ref[R * S :, :] = jnp.zeros((NWIN * S, WL), F32)
    for sp in range(SP):
        flipped = wave_rows(rows_ref, sp).T
        for s2 in range(2):
            table_ref[pl.ds(sp + SP * s2, R, stride=S), :] = flipped[s2 * R : s2 * R + R]


def quarter_tiles(quarter, m):
    tile = quarter * (Q // T) + m
    return tile, tile + HQ // T


def tile_bins(seg_ref, tile, first):
    return jnp.broadcast_to(seg_ref[0:1, pl.ds(pl.multiple_of(tile * T, T), T)], (S, T)) - first


def tile_basis(psi_ref, tile):
    return psi_ref[pl.ds(pl.multiple_of(tile * T, T), T), :]


def forward_kernel(k, edge_ref, seg_ref, table_ref, psi_ref, out_ref):
    quarter = (lax.axis_index("wave") + k) & (NX - 1)

    def select(tile, first, start):
        window = table_ref[pl.ds(pl.multiple_of(first * S, S), NWIN * S), :].astype(BF16)
        fields = lax.dot_general(
            window, tile_basis(psi_ref, tile), (((1,), (1,)), ((), ())), preferred_element_type=F32
        )
        seg = tile_bins(seg_ref, tile, first)
        for g in range(NWIN):
            start = jnp.where(seg == g, fields[g * S : g * S + S], start)
        return start

    def put(m, parts):
        out_ref[:, pl.ds(pl.multiple_of(m * T, T), T)] = jnp.concatenate(parts, axis=0).astype(BF16)

    zero = jnp.zeros((S, T), F32)

    for m in range(HQ // T):
        put(m, [select(tile, edge_ref[tile], zero) for tile in quarter_tiles(quarter, m)])

    @pl.when(edge_ref[2 * TILES + quarter] >= NWIN)
    def _():
        @pl.loop(0, HQ // T)
        def _(m):
            put(
                m,
                [
                    lax.fori_loop(
                        0,
                        edge_ref[TILES + tile] // NWIN + 1,
                        lambda w, acc: select(tile, edge_ref[tile] + w * NWIN, acc),
                        zero,
                    )
                    for tile in quarter_tiles(quarter, m)
                ],
            )


def weight_kernel(a_ref, b_ref, c_ref, d_ref, out_ref):
    field = (a_ref[...].astype(F32) + b_ref[...].astype(F32)) + (c_ref[...].astype(F32) + d_ref[...].astype(F32))
    out_ref[...] = (-2.0 / S * field / (1.0 + field * field)).astype(BF16)


def add_quarter(k, edge_ref, w_ref, seg_ref, psi_ref, sums):
    quarter = (lax.axis_index("wave") - k) & (NX - 1)

    def add(m, half, tile, first):
        weight = w_ref[:, pl.ds(pl.multiple_of(m * T, T), T)].astype(F32)[half * S : half * S + S]
        seg = tile_bins(seg_ref, tile, first)
        spread = jnp.concatenate([jnp.where(seg == g, weight, 0.0) for g in range(NWIN)], axis=0)
        added = jnp.dot(spread.astype(BF16), tile_basis(psi_ref, tile), preferred_element_type=F32)
        sums[pl.ds(pl.multiple_of(first * S, S), NWIN * S), :] += added

    for m in range(HQ // T):
        for half, tile in enumerate(quarter_tiles(quarter, m)):
            add(m, half, tile, edge_ref[tile])

    @pl.when(edge_ref[2 * TILES + quarter] >= NWIN)
    def _():
        @pl.loop(0, HQ // T)
        def _(m):
            for half, tile in enumerate(quarter_tiles(quarter, m)):

                @pl.loop(1, edge_ref[TILES + tile] // NWIN + 1)
                def _(w):
                    add(m, half, tile, edge_ref[tile] + w * NWIN)


def backward_first_kernel(edge_ref, w_ref, seg_ref, psi_ref, sums_ref):
    sums_ref[...] = jnp.zeros_like(sums_ref)
    add_quarter(0, edge_ref, w_ref, seg_ref, psi_ref, sums_ref)


def backward_next_kernel(k, begun_ref, edge_ref, w_ref, seg_ref, psi_ref, sums_ref):
    sums_ref[...] = begun_ref[...]
    add_quarter(k, edge_ref, w_ref, seg_ref, psi_ref, sums_ref)


def backward_last_kernel(k, begun_ref, edge_ref, w_ref, seg_ref, psi_ref, amp_ref, norm_ref, out_ref, sums, rows_ref):
    sums[...] = begun_ref[...]
    add_quarter(k, edge_ref, w_ref, seg_ref, psi_ref, sums)
    rows_ref[...] = amp_ref[...].astype(F32)
    norm = (jnp.concatenate([norm_ref[...]] * 2, axis=0) * (2.0 / S)).T
    for sp in range(SP):
        pair = [sums[pl.ds(sp + SP * s2, R, stride=S), :] for s2 in range(2)]
        flipped = jnp.concatenate(pair, axis=0).T
        for q in range(NW):
            where = pl.ds(q * SP + sp, G, stride=16)
            rows_ref[where, :] = rows_ref[where, :] * norm[q * G : q * G + G] + flipped[q * G : q * G + G]
    out_ref[...] = rows_ref[...].astype(BF16)


def unpack_kernel(r_ref, lat_ref, out_ref):
    for sp in range(SP):
        flipped = wave_rows(r_ref, sp).T
        for s2 in range(2):
            s = sp + SP * s2
            out_ref[s] = flipped[s2 * R : s2 * R + R] + lat_ref[s].astype(F32)


def exchange(x, rows):
    y = lax.all_to_all(x.reshape(G, rows, 128), "event", 0, 0)
    return y.reshape(G * rows, 128)


def shift(x, k):
    return lax.ppermute(x, "wave", [(i, (i + k) % NX) for i in range(NX)])


def vmem(shape, dtype=BF16):
    return pltpu.VMEM(shape, dtype)


def call(kernel, name, out_shape, args, scratch=(), spaces=None, out_specs=None, mib=8, flops=None):
    spaces = spaces or "v" * len(args)
    kept = {"v": pltpu.VMEM, "h": pltpu.HBM}
    args = [pltpu.with_memory_space_constraint(a, kept[c]) if c in kept else a for a, c in zip(args, spaces)]
    return pl.pallas_call(
        kernel,
        out_shape=out_shape,
        in_specs=[{"v": VMEM, "h": ANY, "s": SMEM}[c] for c in spaces],
        out_specs=out_specs or jax.tree.map(lambda _: VMEM, out_shape),
        scratch_shapes=scratch,
        compiler_params=pltpu.CompilerParams(vmem_limit_bytes=mib * 1024 * 1024),
        cost_estimate=flops and pl.CostEstimate(flops=flops, bytes_accessed=1 << 20, transcendentals=0),
        name=name,
    )(*args)


def shards(latent, basis, event_bin, length, amplitude_scale, yield_norm, bin_coords):
    latent = latent.transpose(0, 2, 1)
    packed, coords, lat_kept = call(
        pack_kernel,
        "pack",
        (vmem((G * IN_ROWS, 128)), vmem((2, B), F32), vmem((S, R, WL))),
        (latent, length.T, amplitude_scale.T, bin_coords),
        [
            vmem((R, WL), F32),
            vmem((R, WL), F32),
            vmem((G * IN_ROWS, 128), F32),
            pltpu.SemaphoreType.DMA((4,)),
        ],
        "hhhh",
    )
    kern, amp_out, scale, psi, seg, norm, edges = call(
        gen_kernel,
        "gen",
        (
            vmem((NT, NW, TB, TB)),
            vmem((G * 16, 128)),
            vmem((8, B), F32),
            vmem((E, WL)),
            vmem((1, E), jnp.int32),
            vmem((R, WL), F32),
            jax.ShapeDtypeStruct((2 * TILES + NX,), jnp.int32),
        ),
        (exchange(packed, IN_ROWS), coords, basis, event_bin, yield_norm.T),
        [
            vmem((G * IN_ROWS, 128), F32),
            vmem((2, 8, B), F32),
            vmem((NW, NB, 16, TB)),
            vmem((NW, NB, 16, TB), F32),
            vmem((NW, NB, 8, TB), F32),
            vmem((NW, B, 128), F32),
            vmem((2, NB, 8, TB), F32),
            vmem((2, B, 128), F32),
            pltpu.SMEM((1, E), jnp.int32),
            pltpu.SemaphoreType.DMA((4,)),
        ],
        "vvhhh",
        (VMEM,) * 6 + (SMEM,),
        mib=12,
    )
    amp_in = exchange(amp_out, 16)
    bins = (R + NWIN) * S
    table = call(table_kernel, "table", vmem((bins, WL), F32), (amp_in,), [vmem((G * 16, 128), F32)])

    def forward(k):
        return call(
            functools.partial(forward_kernel, k), "forward", vmem((2 * S, HQ)), (edges, seg, table, psi), spaces="svvv", flops=COST
        )

    others = [shift(forward(k), k) for k in (2, 1, 3)]
    weight = call(weight_kernel, "weight", vmem((2 * S, HQ)), (forward(0), *others))
    sums = call(
        backward_first_kernel, "backward0", vmem((bins, WL), F32), (edges, weight, seg, psi), spaces="svvv", flops=COST
    )
    for k in (3, 1):
        sums = call(
            functools.partial(backward_next_kernel, k),
            "backward1",
            vmem((bins, WL), F32),
            (sums, edges, shift(weight, k), seg, psi),
            spaces="vsvvv",
            flops=COST,
        )
    grad_out = call(
        functools.partial(backward_last_kernel, 2),
        "backward",
        vmem((G * 16, 128)),
        (sums, edges, shift(weight, 2), seg, psi, amp_in, norm),
        [vmem((bins, WL), F32), vmem((G * 16, 128), F32)],
        "vsvvvvv",
        flops=COST,
    )
    pulled = call(
        pull_kernel,
        "pull",
        vmem((G * 16, 128), F32),
        (exchange(grad_out, 16), scale, kern),
        [vmem((NW, NB, 16, TB)), vmem((NW, NB, 16, TB), F32)],
    )
    out = call(
        unpack_kernel,
        "unpack",
        jax.ShapeDtypeStruct((S, R, WL), F32),
        (exchange(pulled, 16), lat_kept),
    )
    return out.transpose(0, 2, 1)


def solution(mesh):
    placed = (
        P(None, "wave", "event"),
        P("event", "wave"),
        P("event", None),
        P("wave", "event"),
        P("wave", "event"),
        P("wave", "event"),
        P(),
    )
    return jax.shard_map(
        shards, mesh=mesh, in_specs=placed, out_specs=P(None, "wave", "event"), check_vma=False
    )
```

```python
import functools
import math

import jax
import jax.numpy as jnp
from jax import lax
from jax.experimental import pallas as pl
from jax.experimental.pallas import tpu as pltpu
from jax.sharding import PartitionSpec as P

F32 = jnp.float32
BF16 = jnp.bfloat16

S, WL, R, B, E, G, NW = 8, 128, 64, 2048, 32768, 32, 4
NX = 4
SP = 4
TB = 256
NB = B // TB
NT = NB + NB * (NB - 1) // 2
IN_ROWS = 24
T = 512
TILES = E // T
COST = 10**9
Q = E // NX
HQ = Q // 2
NWIN = 8
ROOT = math.sqrt(math.log2(math.e))
VMEM = pl.BlockSpec(memory_space=pltpu.VMEM)
SMEM = pl.BlockSpec(memory_space=pltpu.SMEM)
ANY = pl.BlockSpec(memory_space=pl.ANY)


def low_lanes(shape):
    return lax.broadcasted_iota(jnp.int32, shape, len(shape) - 1) < 64


def swap(x):
    return pltpu.roll(x, 64, 1)


def pack_kernel(lat_hbm, len_hbm, amp_hbm, xy_hbm, out_ref, xy_ref, lat_ref, len_ref, amp_ref, rows, sems):
    copies = [
        pltpu.make_async_copy(source, target, sems.at[n])
        for n, (source, target) in enumerate(
            ((lat_hbm, lat_ref), (len_hbm, len_ref), (amp_hbm, amp_ref), (xy_hbm, xy_ref))
        )
    ]
    for one in copies:
        one.start()

    def put(row, value):
        for q in range(NW):
            rows[pl.ds(row(q), G, stride=IN_ROWS), :] = value[q * G : q * G + G]

    copies[0].wait()
    for sp in range(SP):
        pair = jnp.concatenate([lat_ref[sp], lat_ref[sp + SP]], axis=0).astype(F32)
        put(lambda q: q * SP + sp, pair.T)
    copies[1].wait()
    copies[2].wait()
    exact = jnp.concatenate([len_ref[...], amp_ref[...]], axis=0).T
    high = exact.astype(BF16).astype(F32)
    put(lambda q: 16 + q, high)
    put(lambda q: 20 + q, exact - high)
    out_ref[...] = rows[...].astype(BF16)
    copies[3].wait()


def split_pair(a, b):
    low = low_lanes(a.shape)
    return jnp.where(low, a, swap(b)), jnp.where(low, swap(a), b)


def put_vectors(x_ref, q, k, vec):
    hi = vec.astype(BF16)
    lo = (vec - hi.astype(F32)).astype(BF16)
    x_ref[q, k // 2, :, (k % 2) * 128 : (k % 2) * 128 + 128] = jnp.concatenate([hi, lo], axis=0)


def times_tile(x_ref, y_ref, q, i, j, tile, both):
    if both:
        y_ref[q, i] += lax.dot_general(
            x_ref[q, j], tile, (((1,), (1,)), ((), ())), preferred_element_type=F32
        )
    y_ref[q, j] += jnp.dot(x_ref[q, i], tile, preferred_element_type=F32)


def tile_place(t):
    i = t & (NB - 1)
    return i, (i + (t >> 3)) & (NB - 1)


def send_rows(y_ref, scale_ref, out_ref):
    for k in range(B // 128):
        parts = []
        for q in range(NW):
            y = y_ref[q, k // 2, :, (k % 2) * 128 : (k % 2) * 128 + 128]
            parts.append((y[0:8] + y[8:16]) * scale_ref[q : q + 1, k * 128 : k * 128 + 128])
        pair = split_pair(*(jnp.concatenate([y[s2 * SP : s2 * SP + SP] for y in parts], axis=0) for s2 in range(2)))
        for d in range(2):
            out_ref[32 * k + 16 * d : 32 * k + 16 * d + 16, :] = pair[d].astype(out_ref.dtype)


def take_vectors(first, second, k, x_ref, scale_ref):
    pair = split_pair(first, second)
    for q in range(NW):
        vec = jnp.concatenate([one[q * SP : q * SP + SP] for one in pair], axis=0)
        put_vectors(x_ref, q, k, vec * scale_ref[q : q + 1, k * 128 : k * 128 + 128])


def gen_kernel(
    r_ref, xy_ref, basis_hbm, bins_hbm, norm_hbm,
    kern_ref, amp_ref, scale_ref, psi_ref, seg_ref, norm_ref, edge_ref,
    rows_ref, la, x_ref, y_ref, sq_row, sq_col, xy_row, xy_col, bins_ref, sems,
):
    copies = [
        pltpu.make_async_copy(source, target, sems.at[n])
        for n, (source, target) in enumerate(
            ((basis_hbm, psi_ref), (bins_hbm, seg_ref), (norm_hbm, norm_ref), (bins_hbm, bins_ref))
        )
    ]
    for one in copies:
        one.start()
    rows_ref[...] = r_ref[...].astype(F32)
    for k in range(B // 128):
        lanes = slice(k * 128, k * 128 + 128)
        base = 2 * k * IN_ROWS
        pair = split_pair(
            rows_ref[base + 16 : base + 24, :], rows_ref[base + IN_ROWS + 16 : base + IN_ROWS + 24, :]
        )
        for one in range(2):
            la[one, :, lanes] = pair[one]
        for c in range(2):
            row = xy_ref[c : c + 1, lanes] * ROOT
            wide = jnp.broadcast_to(row, (128, 128))
            xy_row[c, k // 2, :, (k % 2) * 128 : (k % 2) * 128 + 128] = wide[0:8]
            xy_col[c, lanes, :] = wide.T
    length = la[0, 0:NW, :] + la[0, NW : 2 * NW, :]
    amp = la[1, 0:NW, :] + la[1, NW : 2 * NW, :]
    scale_ref[NW:8, :] = jnp.zeros((8 - NW, B), F32)
    scale_ref[0:NW, :] = amp * jnp.sqrt(length * math.sqrt(2.0))
    la[0, 0:NW, :] = length * length
    for k in range(B // 128):
        lanes = slice(k * 128, k * 128 + 128)
        base = 2 * k * IN_ROWS
        take_vectors(
            rows_ref[base : base + 16, :], rows_ref[base + IN_ROWS : base + IN_ROWS + 16, :], k, x_ref, scale_ref
        )
        for q in range(NW):
            wide = jnp.broadcast_to(la[0, q : q + 1, lanes], (128, 128))
            sq_row[q, k // 2, :, (k % 2) * 128 : (k % 2) * 128 + 128] = wide[0:8]
            sq_col[q, lanes, :] = wide.T
    y_ref[...] = jnp.zeros_like(y_ref)

    step = 32

    def tile(t, both):
        i, j = tile_place(t)
        row0 = pl.multiple_of(i * TB, TB)
        for st in range(TB // step):
            rows = pl.ds(row0 + st * step, step)
            xc = xy_col[0, rows, :].reshape(step // 8, 8, 128)
            yc = xy_col[1, rows, :].reshape(step // 8, 8, 128)
            near = []
            for c in range(2):
                half = slice(c * 128, c * 128 + 128)
                dx = xc - xy_row[0, j, :, half][None]
                dy = yc - xy_row[1, j, :, half][None]
                near.append(-(dx * dx) - dy * dy)
            made = range(2) if both or 2 * st * step < TB else range(1, 2)
            for q in range(NW):
                sq = sq_col[q, rows, :].reshape(step // 8, 8, 128)
                parts = []
                for c in made:
                    root = lax.rsqrt(sq + sq_row[q, j, :, c * 128 : c * 128 + 128][None])
                    parts.append((root * jnp.exp2(root * root * near[c])).reshape(step, 128).astype(BF16))
                kern_ref[t, q, st * step : st * step + step, made[0] * 128 :] = jnp.concatenate(parts, axis=1)
        if not both:
            for q in range(NW):
                kern_ref[t, q, 128:, 0:128] = kern_ref[t, q, 0:128, 128:].T
        for q in range(NW):
            times_tile(x_ref, y_ref, q, i, j, kern_ref[t, q], both)

    @pl.loop(0, NB, unroll=8)
    def _(t):
        tile(t, False)

    @pl.loop(NB, NT, unroll=14)
    def _(t):
        tile(t, True)

    send_rows(y_ref, scale_ref, amp_ref)
    for one in copies:
        one.wait()

    for quarter in range(NX):
        widest = jnp.int32(0)
        for n in range(quarter * TILES // NX, (quarter + 1) * TILES // NX):
            first = bins_ref[0, n * T]
            span = bins_ref[0, n * T + T - 1] - first
            edge_ref[n] = first
            edge_ref[TILES + n] = span
            widest = jnp.maximum(widest, span)
        edge_ref[2 * TILES + quarter] = widest


def pull_kernel(g_ref, scale_ref, kern_ref, out_ref, x_ref, y_ref):
    for k in range(B // 128):
        a = g_ref[32 * k : 32 * k + 16, :].astype(F32)
        b = g_ref[32 * k + 16 : 32 * k + 32, :].astype(F32)
        take_vectors(a, b, k, x_ref, scale_ref)
    y_ref[...] = jnp.zeros_like(y_ref)

    def tile(t, both):
        i, j = tile_place(t)
        for q in range(NW):
            times_tile(x_ref, y_ref, q, i, j, kern_ref[t, q], both)

    @pl.loop(0, NB, unroll=8)
    def _(t):
        tile(t, False)

    @pl.loop(NB, NT, unroll=28)
    def _(t):
        tile(t, True)

    send_rows(y_ref, scale_ref, out_ref)


def wave_rows(ref, sp):
    return jnp.concatenate([ref[pl.ds(q * SP + sp, G, stride=16), :] for q in range(NW)], axis=0)


def table_kernel(amp_ref, table_ref, rows_ref):
    rows_ref[...] = amp_ref[...].astype(F32)
    table_ref[R * S :, :] = jnp.zeros((NWIN * S, WL), F32)
    for sp in range(SP):
        flipped = wave_rows(rows_ref, sp).T
        for s2 in range(2):
            table_ref[pl.ds(sp + SP * s2, R, stride=S), :] = flipped[s2 * R : s2 * R + R]


def quarter_tiles(quarter, m):
    tile = quarter * (Q // T) + m
    return tile, tile + HQ // T


def tile_bins(seg_ref, tile, first):
    return jnp.broadcast_to(seg_ref[0:1, pl.ds(pl.multiple_of(tile * T, T), T)], (S, T)) - first


def tile_basis(psi_ref, tile):
    return psi_ref[pl.ds(pl.multiple_of(tile * T, T), T), :]


def forward_kernel(k, edge_ref, seg_ref, table_ref, psi_ref, out_ref):
    quarter = (lax.axis_index("wave") + k) & (NX - 1)

    def select(tile, first, start):
        window = table_ref[pl.ds(pl.multiple_of(first * S, S), NWIN * S), :].astype(BF16)
        fields = lax.dot_general(
            window, tile_basis(psi_ref, tile), (((1,), (1,)), ((), ())), preferred_element_type=F32
        )
        seg = tile_bins(seg_ref, tile, first)
        for g in range(NWIN):
            start = jnp.where(seg == g, fields[g * S : g * S + S], start)
        return start

    def put(m, parts):
        out_ref[:, pl.ds(pl.multiple_of(m * T, T), T)] = jnp.concatenate(parts, axis=0).astype(BF16)

    zero = jnp.zeros((S, T), F32)

    for m in range(HQ // T):
        put(m, [select(tile, edge_ref[tile], zero) for tile in quarter_tiles(quarter, m)])

    @pl.when(edge_ref[2 * TILES + quarter] >= NWIN)
    def _():
        @pl.loop(0, HQ // T)
        def _(m):
            put(
                m,
                [
                    lax.fori_loop(
                        0,
                        edge_ref[TILES + tile] // NWIN + 1,
                        lambda w, acc: select(tile, edge_ref[tile] + w * NWIN, acc),
                        zero,
                    )
                    for tile in quarter_tiles(quarter, m)
                ],
            )


def weight_kernel(a_ref, b_ref, c_ref, d_ref, out_ref):
    field = (a_ref[...].astype(F32) + b_ref[...].astype(F32)) + (c_ref[...].astype(F32) + d_ref[...].astype(F32))
    out_ref[...] = (-2.0 / S * field / (1.0 + field * field)).astype(BF16)


def add_quarter(k, edge_ref, w_ref, seg_ref, psi_ref, sums):
    quarter = (lax.axis_index("wave") - k) & (NX - 1)

    def add(m, half, tile, first):
        weight = w_ref[:, pl.ds(pl.multiple_of(m * T, T), T)].astype(F32)[half * S : half * S + S]
        seg = tile_bins(seg_ref, tile, first)
        spread = jnp.concatenate([jnp.where(seg == g, weight, 0.0) for g in range(NWIN)], axis=0)
        added = jnp.dot(spread.astype(BF16), tile_basis(psi_ref, tile), preferred_element_type=F32)
        sums[pl.ds(pl.multiple_of(first * S, S), NWIN * S), :] += added

    for m in range(HQ // T):
        for half, tile in enumerate(quarter_tiles(quarter, m)):
            add(m, half, tile, edge_ref[tile])

    @pl.when(edge_ref[2 * TILES + quarter] >= NWIN)
    def _():
        @pl.loop(0, HQ // T)
        def _(m):
            for half, tile in enumerate(quarter_tiles(quarter, m)):

                @pl.loop(1, edge_ref[TILES + tile] // NWIN + 1)
                def _(w):
                    add(m, half, tile, edge_ref[tile] + w * NWIN)


def backward_first_kernel(edge_ref, w_ref, seg_ref, psi_ref, sums_ref):
    sums_ref[...] = jnp.zeros_like(sums_ref)
    add_quarter(0, edge_ref, w_ref, seg_ref, psi_ref, sums_ref)


def backward_next_kernel(k, begun_ref, edge_ref, w_ref, seg_ref, psi_ref, sums_ref):
    sums_ref[...] = begun_ref[...]
    add_quarter(k, edge_ref, w_ref, seg_ref, psi_ref, sums_ref)


def backward_last_kernel(k, begun_ref, edge_ref, w_ref, seg_ref, psi_ref, amp_ref, norm_ref, out_ref, sums, rows_ref):
    sums[...] = begun_ref[...]
    add_quarter(k, edge_ref, w_ref, seg_ref, psi_ref, sums)
    rows_ref[...] = amp_ref[...].astype(F32)
    norm = (jnp.concatenate([norm_ref[...]] * 2, axis=0) * (2.0 / S)).T
    for sp in range(SP):
        pair = [sums[pl.ds(sp + SP * s2, R, stride=S), :] for s2 in range(2)]
        flipped = jnp.concatenate(pair, axis=0).T
        for q in range(NW):
            where = pl.ds(q * SP + sp, G, stride=16)
            rows_ref[where, :] = rows_ref[where, :] * norm[q * G : q * G + G] + flipped[q * G : q * G + G]
    out_ref[...] = rows_ref[...].astype(BF16)


def unpack_kernel(r_ref, lat_ref, out_ref):
    for sp in range(SP):
        flipped = wave_rows(r_ref, sp).T
        for s2 in range(2):
            s = sp + SP * s2
            out_ref[s] = flipped[s2 * R : s2 * R + R] + lat_ref[s].astype(F32)


def exchange(x, rows):
    y = lax.all_to_all(x.reshape(G, rows, 128), "event", 0, 0)
    return y.reshape(G * rows, 128)


def shift(x, k):
    return lax.ppermute(x, "wave", [(i, (i + k) % NX) for i in range(NX)])


def vmem(shape, dtype=BF16):
    return pltpu.VMEM(shape, dtype)


def call(kernel, name, out_shape, args, scratch=(), spaces=None, out_specs=None, mib=8, flops=None):
    spaces = spaces or "v" * len(args)
    kept = {"v": pltpu.VMEM, "h": pltpu.HBM}
    args = [pltpu.with_memory_space_constraint(a, kept[c]) if c in kept else a for a, c in zip(args, spaces)]
    return pl.pallas_call(
        kernel,
        out_shape=out_shape,
        in_specs=[{"v": VMEM, "h": ANY, "s": SMEM}[c] for c in spaces],
        out_specs=out_specs or jax.tree.map(lambda _: VMEM, out_shape),
        scratch_shapes=scratch,
        compiler_params=pltpu.CompilerParams(vmem_limit_bytes=mib * 1024 * 1024),
        cost_estimate=flops and pl.CostEstimate(flops=flops, bytes_accessed=1 << 20, transcendentals=0),
        name=name,
    )(*args)


def shards(latent, basis, event_bin, length, amplitude_scale, yield_norm, bin_coords):
    latent = latent.transpose(0, 2, 1)
    packed, coords, lat_kept = call(
        pack_kernel,
        "pack",
        (vmem((G * IN_ROWS, 128)), vmem((2, B), F32), vmem((S, R, WL))),
        (latent, length.T, amplitude_scale.T, bin_coords),
        [
            vmem((R, WL), F32),
            vmem((R, WL), F32),
            vmem((G * IN_ROWS, 128), F32),
            pltpu.SemaphoreType.DMA((4,)),
        ],
        "hhhh",
    )
    kern, amp_out, scale, psi, seg, norm, edges = call(
        gen_kernel,
        "gen",
        (
            vmem((NT, NW, TB, TB)),
            vmem((G * 16, 128)),
            vmem((8, B), F32),
            vmem((E, WL)),
            vmem((1, E), jnp.int32),
            vmem((R, WL), F32),
            jax.ShapeDtypeStruct((2 * TILES + NX,), jnp.int32),
        ),
        (exchange(packed, IN_ROWS), coords, basis, event_bin, yield_norm.T),
        [
            vmem((G * IN_ROWS, 128), F32),
            vmem((2, 8, B), F32),
            vmem((NW, NB, 16, TB)),
            vmem((NW, NB, 16, TB), F32),
            vmem((NW, NB, 8, TB), F32),
            vmem((NW, B, 128), F32),
            vmem((2, NB, 8, TB), F32),
            vmem((2, B, 128), F32),
            pltpu.SMEM((1, E), jnp.int32),
            pltpu.SemaphoreType.DMA((4,)),
        ],
        "vvhhh",
        (VMEM,) * 6 + (SMEM,),
        mib=20,
    )
    amp_in = exchange(amp_out, 16)
    bins = (R + NWIN) * S
    table = call(table_kernel, "table", vmem((bins, WL), F32), (amp_in,), [vmem((G * 16, 128), F32)])

    def forward(k):
        return call(
            functools.partial(forward_kernel, k), "forward", vmem((2 * S, HQ)), (edges, seg, table, psi), spaces="svvv", flops=COST
        )

    others = [shift(forward(k), k) for k in (2, 1, 3)]
    weight = call(weight_kernel, "weight", vmem((2 * S, HQ)), (forward(0), *others))
    sums = call(
        backward_first_kernel, "backward0", vmem((bins, WL), F32), (edges, weight, seg, psi), spaces="svvv", flops=COST
    )
    for k in (3, 1):
        sums = call(
            functools.partial(backward_next_kernel, k),
            "backward1",
            vmem((bins, WL), F32),
            (sums, edges, shift(weight, k), seg, psi),
            spaces="vsvvv",
            flops=COST,
        )
    grad_out = call(
        functools.partial(backward_last_kernel, 2),
        "backward",
        vmem((G * 16, 128)),
        (sums, edges, shift(weight, 2), seg, psi, amp_in, norm),
        [vmem((bins, WL), F32), vmem((G * 16, 128), F32)],
        "vsvvvvv",
        flops=COST,
    )
    pulled = call(
        pull_kernel,
        "pull",
        vmem((G * 16, 128), F32),
        (exchange(grad_out, 16), scale, kern),
        [vmem((NW, NB, 16, TB)), vmem((NW, NB, 16, TB), F32)],
    )
    out = call(
        unpack_kernel,
        "unpack",
        jax.ShapeDtypeStruct((S, R, WL), F32),
        (exchange(pulled, 16), lat_kept),
    )
    return out.transpose(0, 2, 1)


def solution(mesh):
    placed = (
        P(None, "wave", "event"),
        P("event", "wave"),
        P("event", None),
        P("wave", "event"),
        P("wave", "event"),
        P("wave", "event"),
        P(),
    )
    return jax.shard_map(
        shards, mesh=mesh, in_specs=placed, out_specs=P(None, "wave", "event"), check_vma=False
    )
```
